256 devices in a mesh: pr: 16 (over x, z_lo, core), pc: 16 (over y, z_hi).
Axes of the slice: x: 4, y: 4, z: 8 (z_hi: 4, z_lo: 2; z = z_hi * 2 + z_lo), core: 2. Of those that a mesh axis runs over, the one named last changes fastest.
Arguments:
- root_inverse: float32 [8192, 8192], P('pr', 'pc'), may hold values from -12 to 12
- panels: float32 [2, 4096, 2048], P(None, 'pr', 'pc'), may hold values from -0.09375 to 0.09375
- child_rows: int32 [2, 16], replicated, may hold values from 0 to 31, as said below
- block_inverse: float32 [2, 2048, 2048], P(None, 'pc', 'pr'), may hold values from -6 to 6
Outputs:
- coupling: float32 [2, 8192, 2048], P(None, 'pc', 'pr')
- diagonal: float32 [2, 2048, 2048], P(None, 'pc', 'pr')
The draws below stay inside these ranges and needn't reach their ends.
Inputs may be any that keep to these rules, and one draw needn't show every extreme that they name: `child_rows`: each row holds 16 distinct block indices in no particular order, always including 0 and 31.
All inputs are finite; a program needn't handle non-finite values.
Results may differ from the reference program's by a relative error of at most 0.0001.
Values sent between devices are 32-bit elements; how exact they have to be, the bound alone decides.
A program may use at most 128 MiB of HBM per device.

```python
import jax
import jax.numpy as jnp
from jax import lax

BLOCK = 256
NBLK = 32
W = 2048
NZ = 16
ROOT = 8192


def draw_root_inverse(key, part):
    key = jax.random.fold_in(key, 3)
    first_key = jax.random.fold_in(key, 0)
    base = jax.random.normal(first_key, (ROOT, ROOT), jnp.float32)
    return (base + base.T) * 0.7071067811865476


def draw_child_rows(key, part):
    key = jax.random.fold_in(key, 7)
    lists = []
    for member in range(2):
        member_key = jax.random.fold_in(key, member)
        first_key, second_key = jax.random.split(member_key)
        middle = jax.random.permutation(first_key, NBLK - 2).astype(jnp.int32) + 1
        chosen = jnp.concatenate([jnp.array([0, NBLK - 1], jnp.int32), middle[:NZ - 2]])
        order = jax.random.permutation(second_key, NZ)
        lists.append(chosen[order])
    return jnp.stack(lists)


def block_levels(key, dims, shards, smallest, high):
    loudness, own = 1.0, jax.random.fold_in(key, 6)
    for dim, blocks in shards:
        steps = jnp.exp(jax.random.uniform(jax.random.fold_in(own, dim), (blocks,), jnp.float32, smallest / len(shards), high / len(shards)))
        loudness = loudness * jnp.repeat(steps, dims[dim] // blocks).reshape([-1 if axis == dim else 1 for axis in range(len(dims))])
    return loudness


def centred(rng, shape, deviation, bound, cuts=(), held_as=jnp.bfloat16):
    level = block_levels(rng, shape, cuts, -0.22, 0.18) if cuts else 1.0
    entries = jax.random.normal(rng, shape, jnp.float32) * deviation * level
    return jnp.minimum(jnp.maximum(entries, -bound), bound).astype(held_as)


def setup_inputs(seed: int = 0) -> dict:
    streams_of = jax.random.split(jax.random.key(seed), 5)
    root_inverse = draw_root_inverse(jax.random.fold_in(streams_of[4], 71), 0)
    panels = centred(streams_of[1], (2, NZ * BLOCK, W), (NZ * BLOCK) ** -0.5, 0.09375, ((1, 16), (2, 16)), jnp.float32)
    child_rows = draw_child_rows(jax.random.fold_in(streams_of[4], 71), 0)
    block_inverse = centred(streams_of[3], (2, W, W), 1.0, 6.0, ((1, 16), (2, 16)), jnp.float32)
    return {"root_inverse": root_inverse, "panels": panels, "child_rows": child_rows, "block_inverse": block_inverse}


def reference(root_inverse, panels, child_rows, block_inverse):
    within = jnp.arange(BLOCK, dtype=jnp.int32)
    couplings = []
    diagonals = []
    for member in range(2):
        row_index = (child_rows[member][:, None].astype(jnp.int32) * BLOCK + within[None, :]).reshape(-1).astype(jnp.int32)
        columns = jnp.take(root_inverse, row_index, axis=1)
        coupling = -jnp.dot(columns, panels[member], precision=lax.Precision.HIGHEST)
        chosen = jnp.take(coupling, row_index, axis=0)
        diagonal = block_inverse[member] - jnp.dot(panels[member].T, chosen, precision=lax.Precision.HIGHEST)
        couplings.append(coupling)
        diagonals.append(diagonal)
    return jnp.stack(couplings), jnp.stack(diagonals)
```

```python
import jax
import jax.numpy as jnp
from jax import lax
from jax.experimental import pallas as pl
from jax.experimental.pallas import tpu as pltpu
from jax.sharding import PartitionSpec as P

BLOCK = 256
MESH = pl.DeviceIdType.MESH
F32 = jnp.float32
BF16 = jnp.bfloat16


def split(value):
    high = value.astype(BF16)
    low = (value - high.astype(F32)).astype(BF16)
    return high, low


def kernel(
    rows_ref, a_ref, p_ref, b_ref, c_out, d_out,
    a1, a2s, a2r, acat, pg, pcat, w, sr, x1, x2, zs, zr,
    c1a, c1b, c2s, c2r, ccat, tw, tr, ts, tf,
    a1_send, a1_recv, a2_send, a2_recv, pz_send, pz_recv, py_send, py_recv,
    sib_send, sib_recv, x1_send, x1_recv, x2_send, x2_recv, z_send, z_recv,
    c1_send, c1_recv, c2_send, c2_recv, tr_send, tr_recv, tf_send, tf_recv,
):
    r = lax.axis_index("pr")
    c = lax.axis_index("pc")
    x, zl, co = r // 4, (r // 2) % 2, r % 2
    y, zh = c // 4, c % 4

    def chip(xx, zz, cc):
        return (xx * 4 + zz * 2 + cc, c)

    c1 = (c1a, c1b)
    sibling = chip(x, zl, 1 - co)
    zpartner = chip(x, 1 - zl, co)
    xright = chip((x + 1) % 4, zl, co)
    xleft = chip((x + 3) % 4, zl, co)

    def remote(src, dst, send, recv, device):
        return pltpu.make_async_remote_copy(
            src_ref=src, dst_ref=dst, send_sem=send, recv_sem=recv,
            device_id=device, device_id_type=MESH,
        )

    def wait_bytes(ref, sem):
        pltpu.make_async_copy(ref, ref, sem).wait()

    barrier = pltpu.get_barrier_semaphore()

    def greet(k, carry):
        pl.semaphore_signal(barrier, inc=1, device_id=((r + k) % 16, c), device_id_type=MESH)
        pl.semaphore_signal(barrier, inc=1, device_id=(r, (c + k) % 16), device_id_type=MESH)
        return carry

    lax.fori_loop(1, 16, greet, 0)

    def greet_senders(k, carry):
        @pl.when((r != c) | (k != c))
        def _():
            pl.semaphore_signal(barrier, inc=1, device_id=(c, k), device_id_type=MESH)

        return carry

    lax.fori_loop(0, 16, greet_senders, 0)

    @pl.when(r == c)
    def _():
        pl.semaphore_wait(barrier, 45)

    @pl.when(r != c)
    def _():
        pl.semaphore_wait(barrier, 46)

    def a_spread(k, carry):
        to = (r + k) % 16
        remote(
            a_ref.at[:, pl.ds(to * 16, 16), :], a1.at[pl.ds(r * 2, 2)],
            a1_send, a1_recv, (to, c),
        ).start()
        return carry

    lax.fori_loop(1, 16, a_spread, 0)

    def p_own(child):
        def along_z(k, carry):
            remote(
                p_ref.at[child], pg.at[c, child], pz_send.at[child],
                pz_recv.at[child, k - 1], (r, y * 4 + (zh + k) % 4),
            ).start()
            return carry

        def along_y(k, carry):
            remote(
                p_ref.at[child], pg.at[c, child], py_send.at[child],
                py_recv.at[child], (r, ((y + k) % 4) * 4 + zh),
            ).start()
            return carry

        lax.fori_loop(1, 4, along_z, 0)
        lax.fori_loop(1, 4, along_y, 0)

    def p_forward(child):
        def piece(k, carry):
            source = y * 4 + (zh + 4 - k) % 4
            wait_bytes(pg.at[source, child], pz_recv.at[child, k - 1])

            def along_y(j, inner):
                remote(
                    pg.at[source, child], pg.at[source, child], py_send.at[child],
                    py_recv.at[child], (r, ((y + j) % 4) * 4 + zh),
                ).start()
                return inner

            lax.fori_loop(1, 4, along_y, 0)
            return carry

        lax.fori_loop(1, 4, piece, 0)

    p_own(0)
    a1[pl.ds(r * 2, 2)] = a_ref[:, pl.ds(r * 16, 16), :]
    pg[c] = p_ref[...]
    wait_bytes(a1.at[pl.ds(0, 30)], a1_recv)

    def a_list(child):
        def place(t, carry):
            a2s[child, t] = -a1[rows_ref[child, t]]
            return carry

        lax.fori_loop(0, 16, place, 0)

        def deal(k, carry):
            to = (r + k) % 16
            remote(
                a2s.at[child, to], a2r.at[child, pl.ds(r * 16, 16), :],
                a2_send.at[child], a2_recv.at[child], (to, c),
            ).start()
            return carry

        lax.fori_loop(1, 16, deal, 0)
        a2r[child, pl.ds(r * 16, 16), :] = a2s[child, r]

    a_list(0)
    p_forward(0)
    a_list(1)
    p_own(1)
    p_forward(1)

    def prepare(child):
        wait_bytes(a2r.at[child, pl.ds(0, 240), :], a2_recv.at[child])
        high, low = split(a2r[child].T)
        acat[child, :, 0:256] = high
        acat[child, :, 256:512] = high
        acat[child, :, 512:768] = low
        wait_bytes(pg.at[pl.ds(0, 12), child], py_recv.at[child])

        def pair(q, carry):
            for half in range(2):
                lanes = pl.ds(half * 128, 128)
                high, low = split(pg[q * 2 + half, child])
                pcat[child, q, 0:256, lanes] = high
                pcat[child, q, 256:512, lanes] = low
                pcat[child, q, 512:768, lanes] = high
            return carry

        lax.fori_loop(0, 8, pair, 0)

    def layer(item):
        return 1 - zl if item % 2 == 0 else zl

    def products(item):
        child = item // 2

        def one(j, carry):
            q = ((x + 6 - j) % 4) * 2 + layer(item)
            result = jnp.dot(acat[child], pcat[child, q], preferred_element_type=F32)
            w[item, j, 0] = result[:, 0:128]
            w[item, j, 1] = result[:, 128:256]
            remote(
                w.at[item, j, 1 - co], sr.at[item, j], sib_send.at[item, j],
                sib_recv.at[item, j], sibling,
            ).start()
            return carry

        lax.fori_loop(0, 4, one, 0)

    def chip_sum(item, j):
        wait_bytes(sr.at[item, j], sib_recv.at[item, j])
        sr[item, j] = sr[item, j] + w[item, j, co]

    def x_first(item):
        chip_sum(item, 0)
        remote(
            sr.at[item, 0, pl.ds(0, 256), :], x1.at[item, 0], x1_send.at[item, 0],
            x1_recv.at[item, 0], xright,
        ).start()
        remote(
            sr.at[item, 0, pl.ds(256, 256), :], x1.at[item, 1], x1_send.at[item, 1],
            x1_recv.at[item, 1], xleft,
        ).start()

    def x_second(item):
        chip_sum(item, 1)
        wait_bytes(x1.at[item, 0], x1_recv.at[item, 0])
        sr[item, 1, 0:256, :] = sr[item, 1, 0:256, :] + x1[item, 0]
        remote(
            sr.at[item, 1], x2.at[item, 0], x2_send.at[item, 0],
            x2_recv.at[item, 0], xright,
        ).start()
        chip_sum(item, 3)
        wait_bytes(x1.at[item, 1], x1_recv.at[item, 1])
        sr[item, 3, 256:512, :] = sr[item, 3, 256:512, :] + x1[item, 1]
        remote(
            sr.at[item, 3], x2.at[item, 1], x2_send.at[item, 1],
            x2_recv.at[item, 1], xleft,
        ).start()

    def x_last(item):
        child = item // 2
        chip_sum(item, 2)
        wait_bytes(x2.at[item, 0], x2_recv.at[item, 0])
        wait_bytes(x2.at[item, 1], x2_recv.at[item, 1])
        total = sr[item, 2] + x2[item, 0] + x2[item, 1]
        if item % 2 == 0:
            zs[child] = total
            remote(
                zs.at[child], zr.at[child], z_send.at[child], z_recv.at[child], zpartner
            ).start()
        else:
            wait_bytes(zr.at[child], z_recv.at[child])
            c_out[child] = (total + zr[child]).reshape(2, BLOCK, 128)

    def c_spread(child):
        def one(k, carry):
            to = (c + k) % 16
            remote(
                c_out.at[child, :, pl.ds(to * 16, 16), :], c1[child].at[pl.ds(c * 2, 2)],
                c1_send.at[child], c1_recv.at[child], (r, to),
            ).start()
            return carry

        lax.fori_loop(1, 16, one, 0)
        c1[child][pl.ds(c * 2, 2)] = c_out[child, :, pl.ds(c * 16, 16), :]

    def c_list(child):
        wait_bytes(c1[child].at[pl.ds(0, 30)], c1_recv.at[child])

        def place(t, carry):
            c2s[child, t] = c1[child][rows_ref[child, t]]
            return carry

        lax.fori_loop(0, 16, place, 0)

        def deal(t, carry):
            source = c2s.at[child, t]
            target = c2r.at[child, pl.ds(c * 16, 16), :]

            @pl.when((r != c) | (t != r))
            def _():
                remote(source, target, c2_send.at[child], c2_recv.at[child], (t, r)).start()

            return carry

        lax.fori_loop(0, 16, deal, 0)

        @pl.when(r == c)
        def _():
            c2r[child, pl.ds(c * 16, 16), :] = c2s[child, r]

    def terms(child):
        @pl.when(r == c)
        def _():
            wait_bytes(c2r.at[child, pl.ds(0, 240), :], c2_recv.at[child])

        @pl.when(r != c)
        def _():
            wait_bytes(c2r.at[child], c2_recv.at[child])

        high, low = split(c2r[child].T)
        ccat[child, :, 0:256] = high
        ccat[child, :, 256:512] = high
        ccat[child, :, 512:768] = low

        def one(q, carry):
            result = jnp.dot(ccat[child], pcat[child, q], preferred_element_type=F32)
            tw[child, 0, q] = result[:, 0:128]
            tw[child, 1, q] = result[:, 128:256]
            return carry

        lax.fori_loop(0, 8, one, 0)
        remote(
            tw.at[child, 1 - co], tr.at[child], tr_send.at[child], tr_recv.at[child], sibling
        ).start()

    def terms_spread(child):
        wait_bytes(tr.at[child], tr_recv.at[child])
        ts[child] = tw[child, co] + tr[child]
        mine = r // 2

        def one(k, carry):
            to = (mine + k) % 8
            remote(
                ts.at[child, to], tf.at[child, mine], tf_send.at[child],
                tf_recv.at[child], (to * 2 + co, c),
            ).start()
            return carry

        lax.fori_loop(1, 8, one, 0)
        tf[child, mine] = ts[child, mine]

    def diagonal(child):
        wait_bytes(tf.at[child, pl.ds(0, 7)], tf_recv.at[child])
        total = tf[child, 0]
        for k in range(1, 8):
            total = total + tf[child, k]
        d_out[child] = b_ref[child] - total

    prepare(0)
    products(0)
    x_first(0)
    products(1)
    x_first(1)
    x_second(0)
    x_second(1)
    prepare(1)
    products(2)
    x_first(2)
    x_last(0)
    products(3)
    x_first(3)
    x_second(2)
    x_last(1)
    c_spread(0)
    x_second(3)
    c_list(0)
    x_last(2)
    terms(0)
    x_last(3)
    c_spread(1)
    terms_spread(0)
    c_list(1)
    terms(1)
    diagonal(0)
    terms_spread(1)
    diagonal(1)

    wait_bytes(a1.at[pl.ds(0, 30)], a1_send)
    for child in range(2):
        wait_bytes(a2r.at[child, pl.ds(0, 240), :], a2_send.at[child])
        wait_bytes(pg.at[pl.ds(0, 3), child], pz_send.at[child])
        wait_bytes(pg.at[pl.ds(0, 12), child], py_send.at[child])
        wait_bytes(zs.at[child], z_send.at[child])
        wait_bytes(c1[child].at[pl.ds(0, 30)], c1_send.at[child])

        @pl.when(r == c)
        def _():
            wait_bytes(c2r.at[child, pl.ds(0, 240), :], c2_send.at[child])

        @pl.when(r != c)
        def _():
            wait_bytes(c2r.at[child], c2_send.at[child])

        wait_bytes(tr.at[child], tr_send.at[child])
        wait_bytes(tf.at[child, pl.ds(0, 7)], tf_send.at[child])
    for item in range(4):
        for j in range(4):
            wait_bytes(sr.at[item, j], sib_send.at[item, j])
        for side in range(2):
            wait_bytes(x1.at[item, side], x1_send.at[item, side])
            wait_bytes(x2.at[item, side], x2_send.at[item, side])


def body(root_inverse, panels, child_rows, block_inverse):
    vmem = pl.BlockSpec(memory_space=pltpu.VMEM)
    dma = pltpu.SemaphoreType.DMA
    coupling, diagonal = pl.pallas_call(
        kernel,
        out_shape=(
            jax.ShapeDtypeStruct((2, 2, BLOCK, 128), F32),
            jax.ShapeDtypeStruct((2, 128, 128), F32),
        ),
        in_specs=[pl.BlockSpec(memory_space=pltpu.SMEM), vmem, vmem, vmem],
        out_specs=(vmem, vmem),
        scratch_shapes=[
            pltpu.VMEM((32, 16, 512), F32),
            pltpu.VMEM((2, 16, 16, 512), F32),
            pltpu.VMEM((2, 256, 512), F32),
            pltpu.VMEM((2, 512, 768), BF16),
            pltpu.VMEM((16, 2, 256, 128), F32),
            pltpu.VMEM((2, 8, 768, 256), BF16),
            pltpu.VMEM((4, 4, 2, 512, 128), F32),
            pltpu.VMEM((4, 4, 512, 128), F32),
            pltpu.VMEM((4, 2, 256, 128), F32),
            pltpu.VMEM((4, 2, 512, 128), F32),
            pltpu.VMEM((2, 512, 128), F32),
            pltpu.VMEM((2, 512, 128), F32),
            pltpu.VMEM((32, 16, 128), F32),
            pltpu.VMEM((32, 16, 128), F32),
            pltpu.VMEM((2, 16, 16, 128), F32),
            pltpu.VMEM((2, 256, 128), F32),
            pltpu.VMEM((2, 128, 768), BF16),
            pltpu.VMEM((2, 2, 8, 128, 128), F32),
            pltpu.VMEM((2, 8, 128, 128), F32),
            pltpu.VMEM((2, 8, 128, 128), F32),
            pltpu.VMEM((2, 8, 128, 128), F32),
            dma, dma,
            dma((2,)), dma((2,)),
            dma((2,)), dma((2, 3)),
            dma((2,)), dma((2,)),
            dma((4, 4)), dma((4, 4)),
            dma((4, 2)), dma((4, 2)),
            dma((4, 2)), dma((4, 2)),
            dma((2,)), dma((2,)),
            dma((2,)), dma((2,)),
            dma((2,)), dma((2,)),
            dma((2,)), dma((2,)),
            dma((2,)), dma((2,)),
        ],
        compiler_params=pltpu.CompilerParams(
            collective_id=0, has_side_effects=True, vmem_limit_bytes=52 * 1024 * 1024
        ),
        cost_estimate=pl.CostEstimate(
            flops=3 * 2 * 2 * 256 * 2048 * (512 + 128), bytes_accessed=4 << 20, transcendentals=0
        ),
    )(child_rows, root_inverse.reshape(2, BLOCK, 512), panels, block_inverse)
    return coupling.reshape(2, 2 * BLOCK, 128), diagonal


def solution(mesh):
    in_specs = (P("pr", "pc"), P(None, "pr", "pc"), P(), P(None, "pc", "pr"))
    out_specs = (P(None, "pc", "pr"), P(None, "pc", "pr"))
    return jax.shard_map(body, mesh=mesh, in_specs=in_specs, out_specs=out_specs, check_vma=False)
```

```python
import jax
import jax.numpy as jnp
from jax import lax
from jax.experimental import pallas as pl
from jax.experimental.pallas import tpu as pltpu
from jax.sharding import PartitionSpec as P

BLOCK = 256
MESH = pl.DeviceIdType.MESH
F32 = jnp.float32
BF16 = jnp.bfloat16


def split(value):
    high = value.astype(BF16)
    low = (value - high.astype(F32)).astype(BF16)
    return high, low


def kernel(
    rows_ref, a_ref, p_ref, b_ref, c_out, d_out,
    a1, a2, acat, pg, pcat, w, sr, x1, x2, zs, zr,
    c1a, c1b, c2, ccat, tw, tr, ts, tf,
    own_sem, a1_send, a1_recv, pa_send, pa_recv, pz_send, pz_recv, pzh_recv,
    py_send, py_recv, pyh_recv,
    sib_send, sib_recv, x1_send, x1_recv, x2_send, x2_recv, z_send, z_recv,
    c1_send, c1_recv, tr_send, tr_recv, tf_send, tf_recv,
):
    r = lax.axis_index("pr")
    c = lax.axis_index("pc")
    x, zl, co = r // 4, (r // 2) % 2, r % 2
    y, zh = c // 4, c % 4

    def chip(xx, zz, cc):
        return (xx * 4 + zz * 2 + cc, c)

    c1 = (c1a, c1b)
    zup, zdown = y * 4 + (zh + 1) % 4, y * 4 + (zh + 3) % 4
    yup, ydown = ((y + 1) % 4) * 4 + zh, ((y + 3) % 4) * 4 + zh
    places = (zh, (zh + 3) % 4, (zh + 1) % 4, (zh + 2) % 4)
    low_half, high_half = pl.ds(0, 128), pl.ds(128, 128)
    sibling = chip(x, zl, 1 - co)
    zpartner = chip(x, 1 - zl, co)
    xright = chip((x + 1) % 4, zl, co)
    xleft = chip((x + 3) % 4, zl, co)

    def remote(src, dst, send, recv, device):
        return pltpu.make_async_remote_copy(
            src_ref=src, dst_ref=dst, send_sem=send, recv_sem=recv,
            device_id=device, device_id_type=MESH,
        )

    def wait_bytes(ref, sem):
        pltpu.make_async_copy(ref, ref, sem).wait()

    barrier = pltpu.get_barrier_semaphore()

    def greet(k, carry):
        pl.semaphore_signal(barrier, inc=1, device_id=((r + k) % 16, c), device_id_type=MESH)
        return carry

    lax.fori_loop(1, 16, greet, 0)
    for plane in (zup, zdown, yup, ydown):
        pl.semaphore_signal(barrier, inc=1, device_id=(r, plane), device_id_type=MESH)

    def greet_senders(k, carry):
        @pl.when((r != c) | (k != c))
        def _():
            pl.semaphore_signal(barrier, inc=1, device_id=(c, k), device_id_type=MESH)

        return carry

    lax.fori_loop(0, 16, greet_senders, 0)

    @pl.when(r == c)
    def _():
        pl.semaphore_wait(barrier, 34)

    @pl.when(r != c)
    def _():
        pl.semaphore_wait(barrier, 35)

    def a_spread():
        lax.fori_loop(1, 16, a_spread_one, 0)

    def a_spread_one(k, carry):
        to = (r + k) % 16
        remote(
            a_ref.at[:, pl.ds(to * 16, 16), :], a1.at[pl.ds(r * 2, 2)],
            a1_send, a1_recv, (to, c),
        ).start()
        return carry


    def p_spread(child):
        def one(k, carry):
            to = (r + k) % 16
            remote(
                p_ref.at[child, pl.ds(to * 16, 16), :], pg.at[c, child, pl.ds(r * 16, 16), :],
                pa_send.at[child], pa_recv.at[child], (to, c),
            ).start()
            return carry

        lax.fori_loop(1, 16, one, 0)

    def p_gathered(child):
        wait_bytes(pg.at[c, child, pl.ds(0, 240), :], pa_recv.at[child])

    def send_piece(piece, child, to, send, recv):
        remote(pg.at[piece, child], pg.at[piece, child], send, recv, (r, to)).start()

    def send_half(piece, child, half, to, send, recv):
        ref = pg.at[piece, child, half, :]
        remote(ref, ref, send, recv, (r, to)).start()

    def p_z(child):
        send_piece(c, child, zup, pz_send.at[child], pz_recv.at[child, 0])
        send_piece(c, child, zdown, pz_send.at[child], pz_recv.at[child, 1])

    def p_y(child, k):
        piece = y * 4 + places[k]
        send_piece(piece, child, yup, py_send.at[child], py_recv.at[child, k, 0])
        send_piece(piece, child, ydown, py_send.at[child], py_recv.at[child, k, 1])

    def p_z_pass(child):
        wait_bytes(pg.at[zdown, child], pz_recv.at[child, 0])
        send_half(zdown, child, low_half, zup, pz_send.at[child], pzh_recv.at[child, 0])
        wait_bytes(pg.at[zup, child], pz_recv.at[child, 1])
        send_half(zup, child, high_half, zdown, pz_send.at[child], pzh_recv.at[child, 1])

    def p_z_last(child):
        piece = y * 4 + places[3]
        wait_bytes(pg.at[piece, child, low_half, :], pzh_recv.at[child, 0])
        wait_bytes(pg.at[piece, child, high_half, :], pzh_recv.at[child, 1])

    def p_y_pass(child, k):
        below, above = ((y + 3) % 4) * 4 + places[k], ((y + 1) % 4) * 4 + places[k]
        wait_bytes(pg.at[below, child], py_recv.at[child, k, 0])
        send_half(below, child, low_half, yup, py_send.at[child], pyh_recv.at[child, k, 0])
        wait_bytes(pg.at[above, child], py_recv.at[child, k, 1])
        send_half(above, child, high_half, ydown, py_send.at[child], pyh_recv.at[child, k, 1])

    def p_y_last(child, k):
        piece = ((y + 2) % 4) * 4 + places[k]
        wait_bytes(pg.at[piece, child, low_half, :], pyh_recv.at[child, k, 0])
        wait_bytes(pg.at[piece, child, high_half, :], pyh_recv.at[child, k, 1])

    a_own = pltpu.make_async_copy(
        a_ref.at[:, pl.ds(r * 16, 16), :], a1.at[pl.ds(r * 2, 2)], own_sem.at[0]
    )
    p_mine = [
        pltpu.make_async_copy(
            p_ref.at[child, pl.ds(r * 16, 16), :], pg.at[c, child, pl.ds(r * 16, 16), :],
            own_sem.at[1 + child],
        )
        for child in range(2)
    ]

    def own():
        for copy in (p_mine[0], p_mine[1], a_own):
            copy.start()

    def own_ready():
        for copy in (p_mine[0], p_mine[1], a_own):
            copy.wait()

    def a_gathered():
        wait_bytes(a1.at[pl.ds(0, 30)], a1_recv)

    def a_list(child):
        for t in range(16):
            a2[child, t * 16:(t + 1) * 16, :] = -a1[rows_ref[child, t]]
        high, low = split(a2[child].T)
        acat[child, :, 0:256] = high
        acat[child, :, 256:512] = high
        acat[child, :, 512:768] = low

    def p_ready(child):
        for k in range(4):
            p_y_last(child, k)

        def pair(q, carry):
            for half in range(2):
                lanes = pl.ds(half * 128, 128)
                high, low = split(pg[q * 2 + half, child])
                pcat[child, q, 0:256, lanes] = high
                pcat[child, q, 256:512, lanes] = low
                pcat[child, q, 512:768, lanes] = high
            return carry

        lax.fori_loop(0, 8, pair, 0)

    def layer(item):
        return 1 - zl if item % 2 == 0 else zl

    def products(item):
        child = item // 2

        def one(j, carry):
            q = ((x + 6 - j) % 4) * 2 + layer(item)
            result = jnp.dot(acat[child], pcat[child, q], preferred_element_type=F32)
            w[item, j, 0] = result[:, 0:128]
            w[item, j, 1] = result[:, 128:256]
            remote(
                w.at[item, j, 1 - co], sr.at[item, j], sib_send.at[item, j],
                sib_recv.at[item, j], sibling,
            ).start()
            return carry

        lax.fori_loop(0, 4, one, 0)

    def chip_sum(item, j):
        wait_bytes(sr.at[item, j], sib_recv.at[item, j])
        sr[item, j] = sr[item, j] + w[item, j, co]

    def x_first(item):
        chip_sum(item, 0)
        remote(
            sr.at[item, 0, pl.ds(0, 256), :], x1.at[item, 0], x1_send.at[item, 0],
            x1_recv.at[item, 0], xright,
        ).start()
        remote(
            sr.at[item, 0, pl.ds(256, 256), :], x1.at[item, 1], x1_send.at[item, 1],
            x1_recv.at[item, 1], xleft,
        ).start()

    def x_second(item):
        chip_sum(item, 1)
        wait_bytes(x1.at[item, 0], x1_recv.at[item, 0])
        sr[item, 1, 0:256, :] = sr[item, 1, 0:256, :] + x1[item, 0]
        remote(
            sr.at[item, 1], x2.at[item, 0], x2_send.at[item, 0],
            x2_recv.at[item, 0], xright,
        ).start()
        chip_sum(item, 3)
        wait_bytes(x1.at[item, 1], x1_recv.at[item, 1])
        sr[item, 3, 256:512, :] = sr[item, 3, 256:512, :] + x1[item, 1]
        remote(
            sr.at[item, 3], x2.at[item, 1], x2_send.at[item, 1],
            x2_recv.at[item, 1], xleft,
        ).start()

    def x_last(item):
        child = item // 2
        chip_sum(item, 2)
        wait_bytes(x2.at[item, 0], x2_recv.at[item, 0])
        wait_bytes(x2.at[item, 1], x2_recv.at[item, 1])
        total = sr[item, 2] + x2[item, 0] + x2[item, 1]
        if item % 2 == 0:
            zs[child] = total
            remote(
                zs.at[child], zr.at[child], z_send.at[child], z_recv.at[child], zpartner
            ).start()
        else:
            wait_bytes(zr.at[child], z_recv.at[child])
            c_out[child] = (total + zr[child]).reshape(2, BLOCK, 128)

    def c_spread(child):
        def one(u, carry):
            source = c_out.at[child, :, pl.ds(u * 16, 16), :]
            target = c1[child].at[pl.ds(c * 2, 2)]

            @pl.when((r != c) | (u != r))
            def _():
                remote(source, target, c1_send.at[child], c1_recv.at[child], (u, r)).start()

            return carry

        lax.fori_loop(0, 16, one, 0)

        @pl.when(r == c)
        def _():
            c1[child][pl.ds(c * 2, 2)] = c_out[child, :, pl.ds(r * 16, 16), :]

    def c_wait(child, sem):
        @pl.when(r == c)
        def _():
            wait_bytes(c1[child].at[pl.ds(0, 30)], sem)

        @pl.when(r != c)
        def _():
            wait_bytes(c1[child], sem)

    def c_ready(child):
        c_wait(child, c1_recv.at[child])
        for t in range(16):
            c2[child, t * 16:(t + 1) * 16, :] = c1[child][rows_ref[child, t]]

    def terms(child):
        high, low = split(c2[child].T)
        ccat[child, :, 0:256] = high
        ccat[child, :, 256:512] = high
        ccat[child, :, 512:768] = low

        def one(q, carry):
            result = jnp.dot(ccat[child], pcat[child, q], preferred_element_type=F32)
            tw[child, 0, q] = result[:, 0:128]
            tw[child, 1, q] = result[:, 128:256]
            return carry

        lax.fori_loop(0, 8, one, 0)
        remote(
            tw.at[child, 1 - co], tr.at[child], tr_send.at[child], tr_recv.at[child], sibling
        ).start()

    def terms_spread(child):
        wait_bytes(tr.at[child], tr_recv.at[child])
        ts[child] = tw[child, co] + tr[child]
        mine = r // 2

        def one(k, carry):
            to = (mine + k) % 8
            remote(
                ts.at[child, to], tf.at[child, mine], tf_send.at[child],
                tf_recv.at[child], (to * 2 + co, c),
            ).start()
            return carry

        lax.fori_loop(1, 8, one, 0)
        tf[child, mine] = ts[child, mine]

    def diagonal(child):
        wait_bytes(tf.at[child, pl.ds(0, 7)], tf_recv.at[child])
        total = tf[child, 0]
        for k in range(1, 8):
            total = total + tf[child, k]
        d_out[child] = b_ref[child] - total

    def a_sent():
        wait_bytes(a1.at[pl.ds(0, 30)], a1_send)

    def p_sent(child):
        wait_bytes(pg.at[c, child, pl.ds(0, 240), :], pa_send.at[child])
        wait_bytes(pg.at[pl.ds(0, 3), child], pz_send.at[child])
        wait_bytes(pg.at[pl.ds(0, 12), child], py_send.at[child])

    def r_sent(child):
        wait_bytes(zs.at[child], z_send.at[child])
        for item in (2 * child, 2 * child + 1):
            for j in range(4):
                wait_bytes(sr.at[item, j], sib_send.at[item, j])
            for side in range(2):
                wait_bytes(x1.at[item, side], x1_send.at[item, side])
                wait_bytes(x2.at[item, side], x2_send.at[item, side])

    def c_sent(child):
        c_wait(child, c1_send.at[child])

    def t_sent(child):
        wait_bytes(tr.at[child], tr_send.at[child])
        wait_bytes(tf.at[child, pl.ds(0, 7)], tf_send.at[child])

    own()
    p_spread(0)
    p_spread(1)
    own_ready()
    p_gathered(0)
    p_z(0)
    p_y(0, 0)
    p_gathered(1)
    p_z(1)
    p_y_pass(0, 0)
    p_z_pass(0)
    a_spread()
    p_y(0, 1)
    p_y(0, 2)
    p_z_last(0)
    p_y(0, 3)
    p_y_pass(0, 1)
    p_y_pass(0, 2)
    p_y_pass(0, 3)
    p_y(1, 0)
    a_gathered()
    a_list(0)
    a_list(1)
    p_ready(0)
    products(0)
    x_first(0)
    p_z_pass(1)
    p_y(1, 1)
    p_y(1, 2)
    products(1)
    x_first(1)
    p_z_last(1)
    p_y(1, 3)
    p_y_pass(1, 0)
    x_second(0)
    p_y_pass(1, 1)
    p_y_pass(1, 2)
    x_second(1)
    x_last(0)
    p_y_pass(1, 3)
    x_last(1)
    c_spread(0)
    p_ready(1)
    products(2)
    x_first(2)
    products(3)
    x_first(3)
    x_second(2)
    c_ready(0)
    x_second(3)
    terms(0)
    x_last(2)
    terms_spread(0)
    x_last(3)
    c_spread(1)
    diagonal(0)
    c_ready(1)
    terms(1)
    terms_spread(1)
    diagonal(1)

    a_sent()
    for child in range(2):
        p_sent(child)
        r_sent(child)
        c_sent(child)
        t_sent(child)


def body(root_inverse, panels, child_rows, block_inverse):
    vmem = pl.BlockSpec(memory_space=pltpu.VMEM)
    hbm = pl.BlockSpec(memory_space=pl.ANY)
    dma = pltpu.SemaphoreType.DMA
    coupling, diagonal = pl.pallas_call(
        kernel,
        out_shape=(
            jax.ShapeDtypeStruct((2, 2, BLOCK, 128), F32),
            jax.ShapeDtypeStruct((2, 128, 128), F32),
        ),
        in_specs=[pl.BlockSpec(memory_space=pltpu.SMEM), hbm, hbm, vmem],
        out_specs=(vmem, vmem),
        scratch_shapes=[
            pltpu.VMEM((32, 16, 512), F32),
            pltpu.VMEM((2, 256, 512), F32),
            pltpu.VMEM((2, 512, 768), BF16),
            pltpu.VMEM((16, 2, 256, 128), F32),
            pltpu.VMEM((2, 8, 768, 256), BF16),
            pltpu.VMEM((4, 4, 2, 512, 128), F32),
            pltpu.VMEM((4, 4, 512, 128), F32),
            pltpu.VMEM((4, 2, 256, 128), F32),
            pltpu.VMEM((4, 2, 512, 128), F32),
            pltpu.VMEM((2, 512, 128), F32),
            pltpu.VMEM((2, 512, 128), F32),
            pltpu.VMEM((32, 16, 128), F32),
            pltpu.VMEM((32, 16, 128), F32),
            pltpu.VMEM((2, 256, 128), F32),
            pltpu.VMEM((2, 128, 768), BF16),
            pltpu.VMEM((2, 2, 8, 128, 128), F32),
            pltpu.VMEM((2, 8, 128, 128), F32),
            pltpu.VMEM((2, 8, 128, 128), F32),
            pltpu.VMEM((2, 8, 128, 128), F32),
            dma((3,)),
            dma, dma,
            dma((2,)), dma((2,)),
            dma((2,)), dma((2, 2)), dma((2, 2)),
            dma((2,)), dma((2, 4, 2)), dma((2, 4, 2)),
            dma((4, 4)), dma((4, 4)),
            dma((4, 2)), dma((4, 2)),
            dma((4, 2)), dma((4, 2)),
            dma((2,)), dma((2,)),
            dma((2,)), dma((2,)),
            dma((2,)), dma((2,)),
            dma((2,)), dma((2,)),
        ],
        compiler_params=pltpu.CompilerParams(
            collective_id=0, has_side_effects=True, vmem_limit_bytes=52 * 1024 * 1024
        ),
        cost_estimate=pl.CostEstimate(
            flops=3 * 2 * 2 * 256 * 2048 * (512 + 128), bytes_accessed=4 << 20, transcendentals=0
        ),
    )(child_rows, root_inverse.reshape(2, BLOCK, 512), panels, block_inverse)
    return coupling.reshape(2, 2 * BLOCK, 128), diagonal


def solution(mesh):
    in_specs = (P("pr", "pc"), P(None, "pr", "pc"), P(), P(None, "pc", "pr"))
    out_specs = (P(None, "pc", "pr"), P(None, "pc", "pr"))
    return jax.shard_map(body, mesh=mesh, in_specs=in_specs, out_specs=out_specs, check_vma=False)
```

```python
import jax
import jax.numpy as jnp
from jax import lax
from jax.experimental import pallas as pl
from jax.experimental.pallas import tpu as pltpu
from jax.sharding import PartitionSpec as P

BLOCK = 256
MESH = pl.DeviceIdType.MESH
F32 = jnp.float32
BF16 = jnp.bfloat16


def split(value):
    high = value.astype(BF16)
    low = (value - high.astype(F32)).astype(BF16)
    return high, low


def kernel(
    rows_ref, a_ref, p_ref, b_ref, c_out, d_out,
    a1, a2, acat, pg, pcat, w, sr, x1, x2, zs, zr, zq,
    c1a, c1b, c2, ccat, tw, tr, ts, tf,
    own_sem, a1_send, a1_recv, pa_send, pa_recv, pz_send, pz_recv, pzh_recv,
    py_send, py_recv, pyh_recv,
    sib_send, sib_recv, x1_send, x1_recv, x2_send, x2_recv, z_send, z_recv, zq_send, zq_recv,
    c1_send, c1_recv, tr_send, tr_recv, tf_send, tf_recv,
):
    r = lax.axis_index("pr")
    c = lax.axis_index("pc")
    x, zl, co = r // 4, (r // 2) % 2, r % 2
    y, zh = c // 4, c % 4

    def chip(xx, zz, cc):
        return (xx * 4 + zz * 2 + cc, c)

    c1 = (c1a, c1b)
    zup, zdown = y * 4 + (zh + 1) % 4, y * 4 + (zh + 3) % 4
    yup, ydown = ((y + 1) % 4) * 4 + zh, ((y + 3) % 4) * 4 + zh
    places = (zh, (zh + 3) % 4, (zh + 1) % 4, (zh + 2) % 4)
    low_half, high_half = pl.ds(0, 128), pl.ds(128, 128)
    sibling = chip(x, zl, 1 - co)
    zpartner = chip(x, 1 - zl, co)
    xright = chip((x + 1) % 4, zl, co)
    xleft = chip((x + 3) % 4, zl, co)

    def remote(src, dst, send, recv, device):
        return pltpu.make_async_remote_copy(
            src_ref=src, dst_ref=dst, send_sem=send, recv_sem=recv,
            device_id=device, device_id_type=MESH,
        )

    def wait_bytes(ref, sem):
        pltpu.make_async_copy(ref, ref, sem).wait()

    barrier = pltpu.get_barrier_semaphore()

    def greet(k, carry):
        pl.semaphore_signal(barrier, inc=1, device_id=((r + k) % 16, c), device_id_type=MESH)
        return carry

    lax.fori_loop(1, 16, greet, 0)
    for plane in (zup, zdown, yup, ydown):
        pl.semaphore_signal(barrier, inc=1, device_id=(r, plane), device_id_type=MESH)

    def greet_senders(k, carry):
        @pl.when((r != c) | (k != c))
        def _():
            pl.semaphore_signal(barrier, inc=1, device_id=(c, k), device_id_type=MESH)

        return carry

    lax.fori_loop(0, 16, greet_senders, 0)

    @pl.when(r == c)
    def _():
        pl.semaphore_wait(barrier, 34)

    @pl.when(r != c)
    def _():
        pl.semaphore_wait(barrier, 35)

    def a_spread():
        lax.fori_loop(1, 16, a_spread_one, 0)

    def a_spread_one(k, carry):
        to = (r + k) % 16
        remote(
            a_ref.at[:, pl.ds(to * 16, 16), :], a1.at[pl.ds(r * 2, 2)],
            a1_send, a1_recv, (to, c),
        ).start()
        return carry


    def p_spread(child):
        def one(k, carry):
            to = (r + k) % 16
            remote(
                p_ref.at[child, pl.ds(to * 16, 16), :], pg.at[c, child, pl.ds(r * 16, 16), :],
                pa_send.at[child], pa_recv.at[child], (to, c),
            ).start()
            return carry

        lax.fori_loop(1, 16, one, 0)

    def p_gathered(child):
        wait_bytes(pg.at[c, child, pl.ds(0, 240), :], pa_recv.at[child])

    def send_piece(piece, child, to, send, recv):
        remote(pg.at[piece, child], pg.at[piece, child], send, recv, (r, to)).start()

    def send_half(piece, child, half, to, send, recv):
        ref = pg.at[piece, child, half, :]
        remote(ref, ref, send, recv, (r, to)).start()

    def p_z(child):
        send_piece(c, child, zup, pz_send.at[child], pz_recv.at[child, 0])
        send_piece(c, child, zdown, pz_send.at[child], pz_recv.at[child, 1])

    def p_y(child, k):
        piece = y * 4 + places[k]
        send_piece(piece, child, yup, py_send.at[child], py_recv.at[child, k, 0])
        send_piece(piece, child, ydown, py_send.at[child], py_recv.at[child, k, 1])

    def p_z_pass(child):
        wait_bytes(pg.at[zdown, child], pz_recv.at[child, 0])
        send_half(zdown, child, low_half, zup, pz_send.at[child], pzh_recv.at[child, 0])
        wait_bytes(pg.at[zup, child], pz_recv.at[child, 1])
        send_half(zup, child, high_half, zdown, pz_send.at[child], pzh_recv.at[child, 1])

    def p_z_last(child):
        piece = y * 4 + places[3]
        wait_bytes(pg.at[piece, child, low_half, :], pzh_recv.at[child, 0])
        wait_bytes(pg.at[piece, child, high_half, :], pzh_recv.at[child, 1])

    def p_y_pass(child, k):
        below, above = ((y + 3) % 4) * 4 + places[k], ((y + 1) % 4) * 4 + places[k]
        wait_bytes(pg.at[below, child], py_recv.at[child, k, 0])
        send_half(below, child, low_half, yup, py_send.at[child], pyh_recv.at[child, k, 0])
        wait_bytes(pg.at[above, child], py_recv.at[child, k, 1])
        send_half(above, child, high_half, ydown, py_send.at[child], pyh_recv.at[child, k, 1])

    def p_y_last(child, k):
        piece = ((y + 2) % 4) * 4 + places[k]
        wait_bytes(pg.at[piece, child, low_half, :], pyh_recv.at[child, k, 0])
        wait_bytes(pg.at[piece, child, high_half, :], pyh_recv.at[child, k, 1])

    a_own = pltpu.make_async_copy(
        a_ref.at[:, pl.ds(r * 16, 16), :], a1.at[pl.ds(r * 2, 2)], own_sem.at[0]
    )
    p_mine = [
        pltpu.make_async_copy(
            p_ref.at[child, pl.ds(r * 16, 16), :], pg.at[c, child, pl.ds(r * 16, 16), :],
            own_sem.at[1 + child],
        )
        for child in range(2)
    ]

    def own():
        for copy in (p_mine[0], p_mine[1], a_own):
            copy.start()

    def own_ready():
        for copy in (p_mine[0], p_mine[1], a_own):
            copy.wait()

    def a_gathered():
        wait_bytes(a1.at[pl.ds(0, 30)], a1_recv)

    def a_list(child):
        for t in range(16):
            a2[child, t * 16:(t + 1) * 16, :] = -a1[rows_ref[child, t]]
        high, low = split(a2[child].T)
        acat[child, :, 0:256] = high
        acat[child, :, 256:512] = high
        acat[child, :, 512:768] = low

    def p_ready(child):
        for k in range(4):
            p_y_last(child, k)

        def pair(q, carry):
            for half in range(2):
                lanes = pl.ds(half * 128, 128)
                high, low = split(pg[q * 2 + half, child])
                pcat[child, q, 0:256, lanes] = high
                pcat[child, q, 256:512, lanes] = low
                pcat[child, q, 512:768, lanes] = high
            return carry

        lax.fori_loop(0, 8, pair, 0)

    z_items = (3,)

    def products(child, layer):
        def one(j, carry):
            q = ((x + 6 - j) % 4) * 2 + (zl + 1 + layer) % 2
            result = jnp.dot(acat[child], pcat[child, q], preferred_element_type=F32)
            for block in range(2):
                item = 2 * child + block
                rows = slice(block * 256, block * 256 + 256)
                w[item, layer, j, 0] = result[rows, 0:128]
                w[item, layer, j, 1] = result[rows, 128:256]
                remote(
                    w.at[item, layer, j, 1 - co], sr.at[item, layer, j], sib_send.at[item, layer, j],
                    sib_recv.at[item, layer, j], sibling,
                ).start()
            return carry

        lax.fori_loop(0, 4, one, 0)

    def chip_sum(item, layer, j):
        wait_bytes(sr.at[item, layer, j], sib_recv.at[item, layer, j])
        total = sr[item, layer, j] + w[item, layer, j, co]
        if item in z_items and layer == 1:
            wait_bytes(zq.at[item, j], zq_recv.at[item, j])
            total = total + zq[item, j]
        sr[item, layer, j] = total

    def z_first(item):
        for j in (0, 1, 3, 2):
            chip_sum(item, 0, j)
            remote(
                sr.at[item, 0, j], zq.at[item, j], zq_send.at[item, j], zq_recv.at[item, j], zpartner
            ).start()

    def x_first(item, layer):
        chip_sum(item, layer, 0)
        for side, rows, to in ((0, pl.ds(0, 128), xright), (1, pl.ds(128, 128), xleft)):
            remote(
                sr.at[item, layer, 0, rows, :], x1.at[item, layer, side],
                x1_send.at[item, layer, side], x1_recv.at[item, layer, side], to,
            ).start()

    def x_second(item, layer):
        for side, j, to in ((0, 1, xright), (1, 3, xleft)):
            chip_sum(item, layer, j)
            rows = slice(side * 128, side * 128 + 128)
            wait_bytes(x1.at[item, layer, side], x1_recv.at[item, layer, side])
            sr[item, layer, j, rows, :] = sr[item, layer, j, rows, :] + x1[item, layer, side]
            remote(
                sr.at[item, layer, j], x2.at[item, layer, side],
                x2_send.at[item, layer, side], x2_recv.at[item, layer, side], to,
            ).start()

    def x_last(item, layer):
        chip_sum(item, layer, 2)
        for side in range(2):
            wait_bytes(x2.at[item, layer, side], x2_recv.at[item, layer, side])
        total = sr[item, layer, 2] + x2[item, layer, 0] + x2[item, layer, 1]
        if layer == 0:
            zs[item] = total
            remote(zs.at[item], zr.at[item], z_send.at[item], z_recv.at[item], zpartner).start()
        else:
            if item not in z_items:
                wait_bytes(zr.at[item], z_recv.at[item])
                total = total + zr[item]
            c_out[item // 2, item % 2] = total

    def c_spread(item):
        child, block = item // 2, item % 2

        def one(k, carry):
            u = (c + k) % 16
            source = c_out.at[child, block, pl.ds(u * 16, 16), :]
            target = c1[child].at[c * 2 + block]

            @pl.when((r != c) | (u != r))
            def _():
                remote(source, target, c1_send.at[child], c1_recv.at[child], (u, r)).start()

            return carry

        lax.fori_loop(0, 16, one, 0)

        @pl.when(r == c)
        def _():
            c1[child][c * 2 + block] = c_out[child, block, pl.ds(r * 16, 16), :]

    def c_wait(child, sem):
        @pl.when(r == c)
        def _():
            wait_bytes(c1[child].at[pl.ds(0, 30)], sem)

        @pl.when(r != c)
        def _():
            wait_bytes(c1[child], sem)

    def c_ready(child):
        c_wait(child, c1_recv.at[child])
        for t in range(16):
            c2[child, t * 16:(t + 1) * 16, :] = c1[child][rows_ref[child, t]]

    def terms(child):
        high, low = split(c2[child].T)
        ccat[child, :, 0:256] = high
        ccat[child, :, 256:512] = high
        ccat[child, :, 512:768] = low

        def one(k, carry):
            q = term_place(k)
            result = jnp.dot(ccat[child], pcat[child, q], preferred_element_type=F32)
            tw[child, q, 0] = result[:, 0:128]
            tw[child, q, 1] = result[:, 128:256]
            remote(
                tw.at[child, q, 1 - co], tr.at[child, q], tr_send.at[child, k],
                tr_recv.at[child, k], sibling,
            ).start()
            return carry

        lax.fori_loop(0, 8, one, 0)

    def term_place(k):
        return ((x + 2 + k) % 4) * 2 + (zl + 1 + k // 4) % 2

    def terms_spread(child):
        for k in (0, 1, 3, 2, 4, 5, 7, 6):
            q = term_place(k)
            wait_bytes(tr.at[child, q], tr_recv.at[child, k])
            total = tw[child, q, co] + tr[child, q]
            if k == 6:
                tf[child, r // 2] = total
            else:
                ts[child, q] = total
                remote(
                    ts.at[child, q], tf.at[child, r // 2], tf_send.at[child],
                    tf_recv.at[child], (q * 2 + co, c),
                ).start()

    def diagonal(child):
        wait_bytes(tf.at[child, pl.ds(0, 7)], tf_recv.at[child])
        total = tf[child, 0]
        for k in range(1, 8):
            total = total + tf[child, k]
        d_out[child] = b_ref[child] - total

    def a_sent():
        wait_bytes(a1.at[pl.ds(0, 30)], a1_send)

    def p_sent(child):
        wait_bytes(pg.at[c, child, pl.ds(0, 240), :], pa_send.at[child])
        wait_bytes(pg.at[pl.ds(0, 3), child], pz_send.at[child])
        wait_bytes(pg.at[pl.ds(0, 12), child], py_send.at[child])

    def r_sent(child):
        for item in (2 * child, 2 * child + 1):
            for layer in range(2):
                for j in range(4):
                    wait_bytes(sr.at[item, layer, j], sib_send.at[item, layer, j])
            if item in z_items:
                for j in range(4):
                    wait_bytes(zq.at[item, j], zq_send.at[item, j])
            else:
                wait_bytes(zs.at[item], z_send.at[item])
            for layer in (1,) if item in z_items else (0, 1):
                for side in range(2):
                    wait_bytes(x1.at[item, layer, side], x1_send.at[item, layer, side])
                    wait_bytes(x2.at[item, layer, side], x2_send.at[item, layer, side])

    def c_sent(child):
        c_wait(child, c1_send.at[child])

    def t_sent(child):
        for k in range(8):
            wait_bytes(tr.at[child, k], tr_send.at[child, k])
        wait_bytes(tf.at[child, pl.ds(0, 7)], tf_send.at[child])

    own()
    p_spread(0)
    p_spread(1)
    own_ready()
    p_gathered(0)
    p_z(0)
    p_y(0, 0)
    p_gathered(1)
    p_z(1)
    p_y_pass(0, 0)
    p_z_pass(0)
    a_spread()
    p_y(0, 1)
    p_y(0, 2)
    p_z_last(0)
    p_y(0, 3)
    p_y_pass(0, 1)
    p_y_pass(0, 2)
    p_y_pass(0, 3)
    p_y(1, 0)
    a_gathered()
    a_list(0)
    a_list(1)
    p_ready(0)
    products(0, 0)
    x_first(0, 0)
    x_first(1, 0)
    p_z_pass(1)
    p_y(1, 1)
    p_y(1, 2)
    products(0, 1)
    x_first(0, 1)
    x_first(1, 1)
    p_z_last(1)
    p_y(1, 3)
    p_y_pass(1, 0)
    x_second(0, 0)
    x_second(1, 0)
    p_y_pass(1, 1)
    p_y_pass(1, 2)
    x_second(0, 1)
    x_second(1, 1)
    x_last(0, 0)
    x_last(1, 0)
    p_y_pass(1, 3)
    x_last(0, 1)
    c_spread(0)
    x_last(1, 1)
    c_spread(1)
    p_ready(1)
    products(1, 0)
    x_first(2, 0)
    z_first(3)
    products(1, 1)
    x_first(2, 1)
    x_first(3, 1)
    x_second(2, 0)
    x_second(2, 1)
    x_second(3, 1)
    x_last(2, 0)
    x_last(2, 1)
    c_spread(2)
    x_last(3, 1)
    c_spread(3)
    c_ready(0)
    terms(0)
    terms_spread(0)
    diagonal(0)
    c_ready(1)
    terms(1)
    terms_spread(1)
    diagonal(1)

    a_sent()
    for child in range(2):
        p_sent(child)
        r_sent(child)
        c_sent(child)
        t_sent(child)


def body(root_inverse, panels, child_rows, block_inverse):
    vmem = pl.BlockSpec(memory_space=pltpu.VMEM)
    hbm = pl.BlockSpec(memory_space=pl.ANY)
    dma = pltpu.SemaphoreType.DMA
    coupling, diagonal = pl.pallas_call(
        kernel,
        out_shape=(
            jax.ShapeDtypeStruct((2, 2, BLOCK, 128), F32),
            jax.ShapeDtypeStruct((2, 128, 128), F32),
        ),
        in_specs=[pl.BlockSpec(memory_space=pltpu.SMEM), hbm, hbm, vmem],
        out_specs=(vmem, vmem),
        scratch_shapes=[
            pltpu.VMEM((32, 16, 512), F32),
            pltpu.VMEM((2, 256, 512), F32),
            pltpu.VMEM((2, 512, 768), BF16),
            pltpu.VMEM((16, 2, 256, 128), F32),
            pltpu.VMEM((2, 8, 768, 256), BF16),
            pltpu.VMEM((4, 2, 4, 2, 256, 128), F32),
            pltpu.VMEM((4, 2, 4, 256, 128), F32),
            pltpu.VMEM((4, 2, 2, 128, 128), F32),
            pltpu.VMEM((4, 2, 2, 256, 128), F32),
            pltpu.VMEM((4, 256, 128), F32),
            pltpu.VMEM((4, 256, 128), F32),
            pltpu.VMEM((4, 4, 256, 128), F32),
            pltpu.VMEM((32, 16, 128), F32),
            pltpu.VMEM((32, 16, 128), F32),
            pltpu.VMEM((2, 256, 128), F32),
            pltpu.VMEM((2, 128, 768), BF16),
            pltpu.VMEM((2, 8, 2, 128, 128), F32),
            pltpu.VMEM((2, 8, 128, 128), F32),
            pltpu.VMEM((2, 8, 128, 128), F32),
            pltpu.VMEM((2, 8, 128, 128), F32),
            dma((3,)),
            dma, dma,
            dma((2,)), dma((2,)),
            dma((2,)), dma((2, 2)), dma((2, 2)),
            dma((2,)), dma((2, 4, 2)), dma((2, 4, 2)),
            dma((4, 2, 4)), dma((4, 2, 4)),
            dma((4, 2, 2)), dma((4, 2, 2)),
            dma((4, 2, 2)), dma((4, 2, 2)),
            dma((4,)), dma((4,)),
            dma((4, 4)), dma((4, 4)),
            dma((2,)), dma((2,)),
            dma((2, 8)), dma((2, 8)),
            dma((2,)), dma((2,)),
        ],
        compiler_params=pltpu.CompilerParams(
            collective_id=0, has_side_effects=True, vmem_limit_bytes=52 * 1024 * 1024
        ),
        cost_estimate=pl.CostEstimate(
            flops=3 * 2 * 2 * 256 * 2048 * (512 + 128), bytes_accessed=4 << 20, transcendentals=0
        ),
    )(child_rows, root_inverse.reshape(2, BLOCK, 512), panels, block_inverse)
    return coupling.reshape(2, 2 * BLOCK, 128), diagonal


def solution(mesh):
    in_specs = (P("pr", "pc"), P(None, "pr", "pc"), P(), P(None, "pc", "pr"))
    out_specs = (P(None, "pc", "pr"), P(None, "pc", "pr"))
    return jax.shard_map(body, mesh=mesh, in_specs=in_specs, out_specs=out_specs, check_vma=False)
```

```python
import jax
import jax.numpy as jnp
from jax import lax
from jax.experimental import pallas as pl
from jax.experimental.pallas import tpu as pltpu
from jax.sharding import PartitionSpec as P

BLOCK = 256
MESH = pl.DeviceIdType.MESH
F32 = jnp.float32
BF16 = jnp.bfloat16


def split(value):
    high = value.astype(BF16)
    low = (value - high.astype(F32)).astype(BF16)
    return high, low


def kernel(
    rows_ref, a_ref, p_ref, b_ref, c_out, d_out, binv,
    a1, a2, acat, pg, pcat, w, sr, x1, x2, zs, zr, zq,
    c1a, c1b, c2, ccat, tw, tr, ts, tf,
    own_sem, a1_send, a1_recv, pa_send, pa_recv, pz_send, pz_recv, pzh_recv,
    py_send, py_recv, pyh_recv,
    sib_send, sib_recv, x1_send, x1_recv, x2_send, x2_recv, z_send, z_recv, zq_send, zq_recv,
    c1_send, c1_recv, tr_send, tr_recv, tf_send, tf_recv,
):
    r = lax.axis_index("pr")
    c = lax.axis_index("pc")
    x, zl, co = r // 4, (r // 2) % 2, r % 2
    y, zh = c // 4, c % 4

    def chip(xx, zz, cc):
        return (xx * 4 + zz * 2 + cc, c)

    c1 = (c1a, c1b)
    zup, zdown = y * 4 + (zh + 1) % 4, y * 4 + (zh + 3) % 4
    yup, ydown = ((y + 1) % 4) * 4 + zh, ((y + 3) % 4) * 4 + zh
    places = (zh, (zh + 3) % 4, (zh + 1) % 4, (zh + 2) % 4)
    low_half, high_half = pl.ds(0, 128), pl.ds(128, 128)
    sibling = chip(x, zl, 1 - co)
    zpartner = chip(x, 1 - zl, co)
    xright = chip((x + 1) % 4, zl, co)
    xleft = chip((x + 3) % 4, zl, co)

    def remote(src, dst, send, recv, device):
        return pltpu.make_async_remote_copy(
            src_ref=src, dst_ref=dst, send_sem=send, recv_sem=recv,
            device_id=device, device_id_type=MESH,
        )

    def wait_bytes(ref, sem):
        pltpu.make_async_copy(ref, ref, sem).wait()

    barrier = pltpu.get_barrier_semaphore()

    def greet(k, carry):
        pl.semaphore_signal(barrier, inc=1, device_id=((r + k) % 16, c), device_id_type=MESH)
        return carry

    lax.fori_loop(1, 16, greet, 0)
    for plane in (zup, zdown, yup, ydown):
        pl.semaphore_signal(barrier, inc=1, device_id=(r, plane), device_id_type=MESH)

    pl.semaphore_wait(barrier, 19)

    def a_spread():
        lax.fori_loop(1, 16, a_spread_one, 0)

    def a_spread_one(k, carry):
        to = (r + k) % 16
        remote(
            a_ref.at[:, pl.ds(to * 16, 16), :], a1.at[pl.ds(r * 2, 2)],
            a1_send, a1_recv, (to, c),
        ).start()
        return carry


    def p_spread(child):
        def one(k, carry):
            to = (r + k) % 16
            remote(
                p_ref.at[child, pl.ds(to * 16, 16), :], pg.at[c, child, pl.ds(r * 16, 16), :],
                pa_send.at[child], pa_recv.at[child], (to, c),
            ).start()
            return carry

        lax.fori_loop(1, 16, one, 0)

    def p_gathered(child):
        wait_bytes(pg.at[c, child, pl.ds(0, 240), :], pa_recv.at[child])

    def send_piece(piece, child, to, send, recv):
        remote(pg.at[piece, child], pg.at[piece, child], send, recv, (r, to)).start()

    def send_half(piece, child, half, to, send, recv):
        ref = pg.at[piece, child, half, :]
        remote(ref, ref, send, recv, (r, to)).start()

    def p_z(child):
        send_piece(c, child, zup, pz_send.at[child], pz_recv.at[child, 0])
        send_piece(c, child, zdown, pz_send.at[child], pz_recv.at[child, 1])

    def p_y(child, k):
        piece = y * 4 + places[k]
        send_piece(piece, child, yup, py_send.at[child], py_recv.at[child, k, 0])
        send_piece(piece, child, ydown, py_send.at[child], py_recv.at[child, k, 1])

    def p_z_pass(child):
        wait_bytes(pg.at[zdown, child], pz_recv.at[child, 0])
        send_half(zdown, child, low_half, zup, pz_send.at[child], pzh_recv.at[child, 0])
        wait_bytes(pg.at[zup, child], pz_recv.at[child, 1])
        send_half(zup, child, high_half, zdown, pz_send.at[child], pzh_recv.at[child, 1])

    def p_z_last(child):
        piece = y * 4 + places[3]
        wait_bytes(pg.at[piece, child, low_half, :], pzh_recv.at[child, 0])
        wait_bytes(pg.at[piece, child, high_half, :], pzh_recv.at[child, 1])

    def p_y_pass(child, k):
        below, above = ((y + 3) % 4) * 4 + places[k], ((y + 1) % 4) * 4 + places[k]
        wait_bytes(pg.at[below, child], py_recv.at[child, k, 0])
        send_half(below, child, low_half, yup, py_send.at[child], pyh_recv.at[child, k, 0])
        wait_bytes(pg.at[above, child], py_recv.at[child, k, 1])
        send_half(above, child, high_half, ydown, py_send.at[child], pyh_recv.at[child, k, 1])

    def p_y_last(child, k):
        piece = ((y + 2) % 4) * 4 + places[k]
        wait_bytes(pg.at[piece, child, low_half, :], pyh_recv.at[child, k, 0])
        wait_bytes(pg.at[piece, child, high_half, :], pyh_recv.at[child, k, 1])

    a_own = pltpu.make_async_copy(
        a_ref.at[:, pl.ds(r * 16, 16), :], a1.at[pl.ds(r * 2, 2)], own_sem.at[0]
    )
    p_mine = [
        pltpu.make_async_copy(
            p_ref.at[child, pl.ds(r * 16, 16), :], pg.at[c, child, pl.ds(r * 16, 16), :],
            own_sem.at[1 + child],
        )
        for child in range(2)
    ]

    b_own = pltpu.make_async_copy(b_ref, binv, own_sem.at[3])

    def own():
        for copy in (p_mine[0], p_mine[1], a_own, b_own):
            copy.start()

    def own_ready():
        for copy in (p_mine[0], p_mine[1], a_own, b_own):
            copy.wait()

    def a_gathered():
        wait_bytes(a1.at[pl.ds(0, 30)], a1_recv)

    def a_list(child):
        for t in range(16):
            a2[child, t * 16:(t + 1) * 16, :] = -a1[rows_ref[child, t]]
        high, low = split(a2[child].T)
        acat[child, :, 0:256] = high
        acat[child, :, 256:512] = high
        acat[child, :, 512:768] = low

    def p_ready(child):
        for k in range(4):
            p_y_last(child, k)

        def pair(q, carry):
            for half in range(2):
                lanes = pl.ds(half * 128, 128)
                high, low = split(pg[q * 2 + half, child])
                pcat[child, q, 0:256, lanes] = high
                pcat[child, q, 256:512, lanes] = low
                pcat[child, q, 512:768, lanes] = high
            return carry

        lax.fori_loop(0, 8, pair, 0)

    z_items = (3,)

    def products(child, layer):
        def one(j, carry):
            product(child, layer, j)
            return carry

        lax.fori_loop(0, 4, one, 0)

    def product(child, layer, j):
        q = ((x + 6 - j) % 4) * 2 + (zl + 1 + layer) % 2
        result = jnp.dot(acat[child], pcat[child, q], preferred_element_type=F32)
        for block in range(2):
            item = 2 * child + block
            rows = slice(block * 256, block * 256 + 256)
            w[item, layer, j, 0] = result[rows, 0:128]
            w[item, layer, j, 1] = result[rows, 128:256]
            remote(
                w.at[item, layer, j, 1 - co], sr.at[item, layer, j], sib_send.at[item, layer, j],
                sib_recv.at[item, layer, j], sibling,
            ).start()

    def products_first(child):
        block_x, block_z = 2 * child, 2 * child + 1
        last = None
        for j in (0, 1, 3, 2):
            product(child, 0, j)
            if last is not None:
                z_send_on(block_z, last)
            if j == 3:
                x_first(block_x, 0)
            last = j
        z_send_on(block_z, last)

    def chip_sum(item, layer, j):
        wait_bytes(sr.at[item, layer, j], sib_recv.at[item, layer, j])
        total = sr[item, layer, j] + w[item, layer, j, co]
        if item in z_items and layer == 1:
            wait_bytes(zq.at[item, j], zq_recv.at[item, j])
            total = total + zq[item, j]
        sr[item, layer, j] = total

    def z_send_on(item, j):
        chip_sum(item, 0, j)
        remote(
            sr.at[item, 0, j], zq.at[item, j], zq_send.at[item, j], zq_recv.at[item, j], zpartner
        ).start()

    def x_first(item, layer):
        chip_sum(item, layer, 0)
        for side, rows, to in ((0, pl.ds(0, 128), xright), (1, pl.ds(128, 128), xleft)):
            remote(
                sr.at[item, layer, 0, rows, :], x1.at[item, layer, side],
                x1_send.at[item, layer, side], x1_recv.at[item, layer, side], to,
            ).start()

    def x_second(item, layer):
        for side, j, to in ((0, 1, xright), (1, 3, xleft)):
            chip_sum(item, layer, j)
            rows = slice(side * 128, side * 128 + 128)
            wait_bytes(x1.at[item, layer, side], x1_recv.at[item, layer, side])
            sr[item, layer, j, rows, :] = sr[item, layer, j, rows, :] + x1[item, layer, side]
            remote(
                sr.at[item, layer, j], x2.at[item, layer, side],
                x2_send.at[item, layer, side], x2_recv.at[item, layer, side], to,
            ).start()

    def x_last(item, layer):
        chip_sum(item, layer, 2)
        for side in range(2):
            wait_bytes(x2.at[item, layer, side], x2_recv.at[item, layer, side])
        total = sr[item, layer, 2] + x2[item, layer, 0] + x2[item, layer, 1]
        if layer == 0:
            zs[item] = total
            remote(zs.at[item], zr.at[item], z_send.at[item], z_recv.at[item], zpartner).start()
        else:
            if item not in z_items:
                wait_bytes(zr.at[item], z_recv.at[item])
                total = total + zr[item]
            c_out[item // 2, item % 2] = total

    def c_spread(item):
        child, block = item // 2, item % 2

        def one(k, carry):
            u = (c + k) % 16
            source = c_out.at[child, block, pl.ds(u * 16, 16), :]
            target = c1[child].at[c * 2 + block]

            @pl.when((r != c) | (u != r))
            def _():
                remote(source, target, c1_send.at[child], c1_recv.at[child], (u, r)).start()

            return carry

        lax.fori_loop(0, 16, one, 0)

        @pl.when(r == c)
        def _():
            c1[child][c * 2 + block] = c_out[child, block, pl.ds(r * 16, 16), :]

    def c_wait(child, sem):
        @pl.when(r == c)
        def _():
            wait_bytes(c1[child].at[pl.ds(0, 30)], sem)

        @pl.when(r != c)
        def _():
            wait_bytes(c1[child], sem)

    def c_ready(child):
        c_wait(child, c1_recv.at[child])
        for t in range(16):
            c2[child, t * 16:(t + 1) * 16, :] = c1[child][rows_ref[child, t]]

    def terms(child):
        high, low = split(c2[child].T)
        ccat[child, :, 0:256] = high
        ccat[child, :, 256:512] = high
        ccat[child, :, 512:768] = low

        def one(k, carry):
            q = term_place(k)
            result = jnp.dot(ccat[child], pcat[child, q], preferred_element_type=F32)
            tw[child, q, 0] = result[:, 0:128]
            tw[child, q, 1] = result[:, 128:256]
            remote(
                tw.at[child, q, 1 - co], tr.at[child, q], tr_send.at[child, k],
                tr_recv.at[child, k], sibling,
            ).start()
            return carry

        lax.fori_loop(0, 8, one, 0)

    def term_place(k):
        return ((x + 2 + k) % 4) * 2 + (zl + 1 + k // 4) % 2

    def terms_spread(child):
        for k in (0, 1, 3, 2, 4, 5, 7, 6):
            q = term_place(k)
            wait_bytes(tr.at[child, q], tr_recv.at[child, k])
            total = tw[child, q, co] + tr[child, q]
            if k == 6:
                tf[child, r // 2] = total
            else:
                ts[child, q] = total
                remote(
                    ts.at[child, q], tf.at[child, r // 2], tf_send.at[child],
                    tf_recv.at[child], (q * 2 + co, c),
                ).start()

    def diagonal(child):
        wait_bytes(tf.at[child, pl.ds(0, 7)], tf_recv.at[child])
        total = tf[child, 0]
        for k in range(1, 8):
            total = total + tf[child, k]
        d_out[child] = binv[child] - total

    def a_sent():
        wait_bytes(a1.at[pl.ds(0, 30)], a1_send)

    def p_sent(child):
        wait_bytes(pg.at[c, child, pl.ds(0, 240), :], pa_send.at[child])
        wait_bytes(pg.at[pl.ds(0, 3), child], pz_send.at[child])
        wait_bytes(pg.at[pl.ds(0, 12), child], py_send.at[child])

    def r_sent(child):
        for item in (2 * child, 2 * child + 1):
            for layer in range(2):
                for j in range(4):
                    wait_bytes(sr.at[item, layer, j], sib_send.at[item, layer, j])
            if item in z_items:
                for j in range(4):
                    wait_bytes(zq.at[item, j], zq_send.at[item, j])
            else:
                wait_bytes(zs.at[item], z_send.at[item])
            for layer in (1,) if item in z_items else (0, 1):
                for side in range(2):
                    wait_bytes(x1.at[item, layer, side], x1_send.at[item, layer, side])
                    wait_bytes(x2.at[item, layer, side], x2_send.at[item, layer, side])

    def c_sent(child):
        c_wait(child, c1_send.at[child])

    def t_sent(child):
        for k in range(8):
            wait_bytes(tr.at[child, k], tr_send.at[child, k])
        wait_bytes(tf.at[child, pl.ds(0, 7)], tf_send.at[child])

    own()
    p_spread(0)
    p_spread(1)
    own_ready()
    p_gathered(0)
    p_z(0)
    p_y(0, 0)
    p_gathered(1)
    p_z(1)
    p_y_pass(0, 0)
    p_z_pass(0)
    a_spread()
    p_y(0, 1)
    p_y(0, 2)
    p_z_last(0)
    p_y(0, 3)
    p_y_pass(0, 1)
    p_y_pass(0, 2)
    p_y_pass(0, 3)
    p_y(1, 0)
    a_gathered()
    a_list(0)
    a_list(1)
    p_z_pass(1)
    p_y(1, 1)
    p_y(1, 2)
    p_ready(0)
    products(0, 0)
    x_first(0, 0)
    x_first(1, 0)
    products(0, 1)
    x_first(0, 1)
    x_first(1, 1)
    p_z_last(1)
    p_y(1, 3)
    p_y_pass(1, 0)
    x_second(0, 0)
    x_second(1, 0)
    p_y_pass(1, 1)
    p_y_pass(1, 2)
    x_second(0, 1)
    x_second(1, 1)
    x_last(0, 0)
    x_last(1, 0)
    p_y_pass(1, 3)
    x_last(0, 1)
    c_spread(0)
    x_last(1, 1)
    c_spread(1)
    p_ready(1)
    products_first(1)
    products(1, 1)
    x_first(2, 1)
    x_first(3, 1)
    x_second(2, 0)
    x_second(2, 1)
    x_second(3, 1)
    x_last(2, 0)
    x_last(2, 1)
    c_spread(2)
    x_last(3, 1)
    c_spread(3)
    c_ready(0)
    terms(0)
    terms_spread(0)
    diagonal(0)
    c_ready(1)
    terms(1)
    terms_spread(1)
    diagonal(1)

    a_sent()
    for child in range(2):
        p_sent(child)
        r_sent(child)
        c_sent(child)
        t_sent(child)


def body(root_inverse, panels, child_rows, block_inverse):
    vmem = pl.BlockSpec(memory_space=pltpu.VMEM)
    hbm = pl.BlockSpec(memory_space=pl.ANY)
    dma = pltpu.SemaphoreType.DMA
    coupling, diagonal = pl.pallas_call(
        kernel,
        out_shape=(
            jax.ShapeDtypeStruct((2, 2, BLOCK, 128), F32),
            jax.ShapeDtypeStruct((2, 128, 128), F32),
        ),
        in_specs=[pl.BlockSpec(memory_space=pltpu.SMEM), hbm, hbm, hbm],
        out_specs=(vmem, vmem),
        scratch_shapes=[
            pltpu.VMEM((2, 128, 128), F32),
            pltpu.VMEM((32, 16, 512), F32),
            pltpu.VMEM((2, 256, 512), F32),
            pltpu.VMEM((2, 512, 768), BF16),
            pltpu.VMEM((16, 2, 256, 128), F32),
            pltpu.VMEM((2, 8, 768, 256), BF16),
            pltpu.VMEM((4, 2, 4, 2, 256, 128), F32),
            pltpu.VMEM((4, 2, 4, 256, 128), F32),
            pltpu.VMEM((4, 2, 2, 128, 128), F32),
            pltpu.VMEM((4, 2, 2, 256, 128), F32),
            pltpu.VMEM((4, 256, 128), F32),
            pltpu.VMEM((4, 256, 128), F32),
            pltpu.VMEM((4, 4, 256, 128), F32),
            pltpu.VMEM((32, 16, 128), F32),
            pltpu.VMEM((32, 16, 128), F32),
            pltpu.VMEM((2, 256, 128), F32),
            pltpu.VMEM((2, 128, 768), BF16),
            pltpu.VMEM((2, 8, 2, 128, 128), F32),
            pltpu.VMEM((2, 8, 128, 128), F32),
            pltpu.VMEM((2, 8, 128, 128), F32),
            pltpu.VMEM((2, 8, 128, 128), F32),
            dma((4,)),
            dma, dma,
            dma((2,)), dma((2,)),
            dma((2,)), dma((2, 2)), dma((2, 2)),
            dma((2,)), dma((2, 4, 2)), dma((2, 4, 2)),
            dma((4, 2, 4)), dma((4, 2, 4)),
            dma((4, 2, 2)), dma((4, 2, 2)),
            dma((4, 2, 2)), dma((4, 2, 2)),
            dma((4,)), dma((4,)),
            dma((4, 4)), dma((4, 4)),
            dma((2,)), dma((2,)),
            dma((2, 8)), dma((2, 8)),
            dma((2,)), dma((2,)),
        ],
        compiler_params=pltpu.CompilerParams(
            collective_id=0, has_side_effects=True, vmem_limit_bytes=63 * 1024 * 1024
        ),
        cost_estimate=pl.CostEstimate(
            flops=3 * 2 * 2 * 256 * 2048 * (512 + 128), bytes_accessed=4 << 20, transcendentals=0
        ),
    )(child_rows, root_inverse.reshape(2, BLOCK, 512), panels, block_inverse)
    return coupling.reshape(2, 2 * BLOCK, 128), diagonal


def solution(mesh):
    in_specs = (P("pr", "pc"), P(None, "pr", "pc"), P(), P(None, "pc", "pr"))
    out_specs = (P(None, "pc", "pr"), P(None, "pc", "pr"))
    return jax.shard_map(body, mesh=mesh, in_specs=in_specs, out_specs=out_specs, check_vma=False)
```

```python
import jax
import jax.numpy as jnp
from jax import lax
from jax.experimental import pallas as pl
from jax.experimental.pallas import tpu as pltpu
from jax.sharding import PartitionSpec as P

BLOCK = 256
MESH = pl.DeviceIdType.MESH
F32 = jnp.float32
BF16 = jnp.bfloat16


def split(value):
    high = value.astype(BF16)
    low = (value - high.astype(F32)).astype(BF16)
    return high, low


def kernel(
    rows_ref, a_ref, p_ref, b_ref, c_out, d_out, binv,
    a1, a2, acat, pg, pcat, w, sr, x1, x2, zs, zr, zq,
    c1a, c1b, c2, ccat, tw, tr, ts, tf,
    own_sem, a1_send, a1_recv, pa_send, pa_recv, pz_send, pz_recv, pzh_recv,
    py_send, py_recv, pyh_recv,
    sib_send, sib_recv, x1_send, x1_recv, x2_send, x2_recv, z_send, z_recv, zq_send, zq_recv,
    c1_send, c1_recv, tr_send, tr_recv, tf_send, tf_recv,
):
    r = lax.axis_index("pr")
    c = lax.axis_index("pc")
    x, zl, co = r // 4, (r // 2) % 2, r % 2
    y, zh = c // 4, c % 4

    def chip(xx, zz, cc):
        return (xx * 4 + zz * 2 + cc, c)

    c1 = (c1a, c1b)
    zup, zdown = y * 4 + (zh + 1) % 4, y * 4 + (zh + 3) % 4
    yup, ydown = ((y + 1) % 4) * 4 + zh, ((y + 3) % 4) * 4 + zh
    places = (zh, (zh + 3) % 4, (zh + 1) % 4, (zh + 2) % 4)
    low_half, high_half = pl.ds(0, 128), pl.ds(128, 128)
    sibling = chip(x, zl, 1 - co)
    zpartner = chip(x, 1 - zl, co)
    xright = chip((x + 1) % 4, zl, co)
    xleft = chip((x + 3) % 4, zl, co)

    def remote(src, dst, send, recv, device):
        return pltpu.make_async_remote_copy(
            src_ref=src, dst_ref=dst, send_sem=send, recv_sem=recv,
            device_id=device, device_id_type=MESH,
        )

    def wait_bytes(ref, sem):
        pltpu.make_async_copy(ref, ref, sem).wait()

    barrier = pltpu.get_barrier_semaphore()

    def greet(k, carry):
        pl.semaphore_signal(barrier, inc=1, device_id=((r + k) % 16, c), device_id_type=MESH)
        return carry

    lax.fori_loop(1, 16, greet, 0)
    for plane in (zup, zdown, yup, ydown):
        pl.semaphore_signal(barrier, inc=1, device_id=(r, plane), device_id_type=MESH)

    pl.semaphore_wait(barrier, 19)

    def a_spread():
        lax.fori_loop(1, 16, a_spread_one, 0)

    def a_spread_one(k, carry):
        to = (r + k) % 16
        remote(
            a_ref.at[:, pl.ds(to * 16, 16), :], a1.at[pl.ds(r * 2, 2)],
            a1_send, a1_recv, (to, c),
        ).start()
        return carry


    def p_spread(child):
        def one(k, carry):
            to = (r + k) % 16
            remote(
                p_ref.at[child, pl.ds(to * 16, 16), :], pg.at[c, child, pl.ds(r * 16, 16), :],
                pa_send.at[child], pa_recv.at[child], (to, c),
            ).start()
            return carry

        lax.fori_loop(1, 16, one, 0)

    def p_gathered(child):
        wait_bytes(pg.at[c, child, pl.ds(0, 240), :], pa_recv.at[child])

    def send_piece(piece, child, to, send, recv):
        remote(pg.at[piece, child], pg.at[piece, child], send, recv, (r, to)).start()

    def send_half(piece, child, half, to, send, recv):
        ref = pg.at[piece, child, half, :]
        remote(ref, ref, send, recv, (r, to)).start()

    def p_z(child):
        send_piece(c, child, zup, pz_send.at[child], pz_recv.at[child, 0])
        send_piece(c, child, zdown, pz_send.at[child], pz_recv.at[child, 1])

    def p_y(child, k):
        piece = y * 4 + places[k]
        send_piece(piece, child, yup, py_send.at[child], py_recv.at[child, k, 0])
        send_piece(piece, child, ydown, py_send.at[child], py_recv.at[child, k, 1])

    def p_z_pass(child):
        wait_bytes(pg.at[zdown, child], pz_recv.at[child, 0])
        send_half(zdown, child, low_half, zup, pz_send.at[child], pzh_recv.at[child, 0])
        wait_bytes(pg.at[zup, child], pz_recv.at[child, 1])
        send_half(zup, child, high_half, zdown, pz_send.at[child], pzh_recv.at[child, 1])

    def p_z_last(child):
        piece = y * 4 + places[3]
        wait_bytes(pg.at[piece, child, low_half, :], pzh_recv.at[child, 0])
        wait_bytes(pg.at[piece, child, high_half, :], pzh_recv.at[child, 1])

    def p_y_pass(child, k):
        below, above = ((y + 3) % 4) * 4 + places[k], ((y + 1) % 4) * 4 + places[k]
        wait_bytes(pg.at[below, child], py_recv.at[child, k, 0])
        send_half(below, child, low_half, yup, py_send.at[child], pyh_recv.at[child, k, 0])
        wait_bytes(pg.at[above, child], py_recv.at[child, k, 1])
        send_half(above, child, high_half, ydown, py_send.at[child], pyh_recv.at[child, k, 1])

    def p_y_last(child, k):
        piece = ((y + 2) % 4) * 4 + places[k]
        wait_bytes(pg.at[piece, child, low_half, :], pyh_recv.at[child, k, 0])
        wait_bytes(pg.at[piece, child, high_half, :], pyh_recv.at[child, k, 1])

    a_own = pltpu.make_async_copy(
        a_ref.at[:, pl.ds(r * 16, 16), :], a1.at[pl.ds(r * 2, 2)], own_sem.at[0]
    )
    p_mine = [
        pltpu.make_async_copy(
            p_ref.at[child, pl.ds(r * 16, 16), :], pg.at[c, child, pl.ds(r * 16, 16), :],
            own_sem.at[1 + child],
        )
        for child in range(2)
    ]

    b_own = pltpu.make_async_copy(b_ref, binv, own_sem.at[3])

    def own():
        for copy in (p_mine[0], p_mine[1], a_own, b_own):
            copy.start()

    def own_ready():
        for copy in (p_mine[0], p_mine[1], a_own, b_own):
            copy.wait()

    def a_gathered():
        wait_bytes(a1.at[pl.ds(0, 30)], a1_recv)

    def a_list(child):
        for t in range(16):
            a2[child, t * 16:(t + 1) * 16, :] = -a1[rows_ref[child, t]]
        high, low = split(a2[child].T)
        acat[child, :, 0:256] = high
        acat[child, :, 256:512] = high
        acat[child, :, 512:768] = low

    def p_ready(child):
        for k in range(4):
            p_y_last(child, k)

        def pair(q, carry):
            for half in range(2):
                lanes = pl.ds(half * 128, 128)
                high, low = split(pg[q * 2 + half, child])
                pcat[child, q, 0:256, lanes] = high
                pcat[child, q, 256:512, lanes] = low
                pcat[child, q, 512:768, lanes] = high
            return carry

        lax.fori_loop(0, 8, pair, 0)

    z_items = (1, 3)

    def products(child, layer):
        def one(j, carry):
            product(child, layer, j)
            return carry

        lax.fori_loop(0, 4, one, 0)

    def product(child, layer, j):
        q = ((x + 6 - j) % 4) * 2 + (zl + 1 + layer) % 2
        result = jnp.dot(acat[child], pcat[child, q], preferred_element_type=F32)
        for block in range(2):
            item = 2 * child + block
            rows = slice(block * 256, block * 256 + 256)
            w[item, layer, j, 0] = result[rows, 0:128]
            w[item, layer, j, 1] = result[rows, 128:256]
            remote(
                w.at[item, layer, j, 1 - co], sr.at[item, layer, j], sib_send.at[item, layer, j],
                sib_recv.at[item, layer, j], sibling,
            ).start()

    def products_first(child):
        block_x, block_z = 2 * child, 2 * child + 1
        last = None
        for j in (0, 1, 3, 2):
            product(child, 0, j)
            if last is not None:
                z_send_on(block_z, last)
            if j == 3:
                x_first(block_x, 0)
            last = j
        z_send_on(block_z, last)

    def chip_sum(item, layer, j):
        wait_bytes(sr.at[item, layer, j], sib_recv.at[item, layer, j])
        total = sr[item, layer, j] + w[item, layer, j, co]
        if item in z_items and layer == 1:
            wait_bytes(zq.at[item, j], zq_recv.at[item, j])
            total = total + zq[item, j]
        sr[item, layer, j] = total

    def z_send_on(item, j):
        chip_sum(item, 0, j)
        remote(
            sr.at[item, 0, j], zq.at[item, j], zq_send.at[item, j], zq_recv.at[item, j], zpartner
        ).start()

    def x_first(item, layer):
        chip_sum(item, layer, 0)
        for side, rows, to in ((0, pl.ds(0, 128), xright), (1, pl.ds(128, 128), xleft)):
            remote(
                sr.at[item, layer, 0, rows, :], x1.at[item, layer, side],
                x1_send.at[item, layer, side], x1_recv.at[item, layer, side], to,
            ).start()

    def x_second(item, layer):
        for side, j, to in ((0, 1, xright), (1, 3, xleft)):
            chip_sum(item, layer, j)
            rows = slice(side * 128, side * 128 + 128)
            wait_bytes(x1.at[item, layer, side], x1_recv.at[item, layer, side])
            sr[item, layer, j, rows, :] = sr[item, layer, j, rows, :] + x1[item, layer, side]
            remote(
                sr.at[item, layer, j], x2.at[item, layer, side],
                x2_send.at[item, layer, side], x2_recv.at[item, layer, side], to,
            ).start()

    def x_last(item, layer):
        chip_sum(item, layer, 2)
        for side in range(2):
            wait_bytes(x2.at[item, layer, side], x2_recv.at[item, layer, side])
        total = sr[item, layer, 2] + x2[item, layer, 0] + x2[item, layer, 1]
        if layer == 0:
            zs[item] = total
            remote(zs.at[item], zr.at[item], z_send.at[item], z_recv.at[item], zpartner).start()
        else:
            if item not in z_items:
                wait_bytes(zr.at[item], z_recv.at[item])
                total = total + zr[item]
            c_out[item // 2, item % 2] = total

    def c_spread(item):
        child, block = item // 2, item % 2

        def one(k, carry):
            u = (c + k) % 16
            source = c_out.at[child, block, pl.ds(u * 16, 16), :]
            target = c1[child].at[c * 2 + block]

            @pl.when((r != c) | (u != r))
            def _():
                remote(source, target, c1_send.at[child], c1_recv.at[child], (u, r)).start()

            return carry

        lax.fori_loop(0, 16, one, 0)

        @pl.when(r == c)
        def _():
            c1[child][c * 2 + block] = c_out[child, block, pl.ds(r * 16, 16), :]

    def c_wait(child, sem):
        @pl.when(r == c)
        def _():
            wait_bytes(c1[child].at[pl.ds(0, 30)], sem)

        @pl.when(r != c)
        def _():
            wait_bytes(c1[child], sem)

    def c_ready(child):
        c_wait(child, c1_recv.at[child])
        for t in range(16):
            c2[child, t * 16:(t + 1) * 16, :] = c1[child][rows_ref[child, t]]

    def terms(child):
        high, low = split(c2[child].T)
        ccat[child, :, 0:256] = high
        ccat[child, :, 256:512] = high
        ccat[child, :, 512:768] = low

        def one(k, carry):
            q = term_place(k)
            result = jnp.dot(ccat[child], pcat[child, q], preferred_element_type=F32)
            tw[child, q, 0] = result[:, 0:128]
            tw[child, q, 1] = result[:, 128:256]
            remote(
                tw.at[child, q, 1 - co], tr.at[child, q], tr_send.at[child, k],
                tr_recv.at[child, k], sibling,
            ).start()
            return carry

        lax.fori_loop(0, 8, one, 0)

    def term_place(k):
        return ((x + 2 + k) % 4) * 2 + (zl + 1 + k // 4) % 2

    def terms_spread(child):
        for k in (0, 1, 3, 2, 4, 5, 7, 6):
            q = term_place(k)
            wait_bytes(tr.at[child, q], tr_recv.at[child, k])
            total = tw[child, q, co] + tr[child, q]
            if k == 6:
                tf[child, r // 2] = total
            else:
                ts[child, q] = total
                remote(
                    ts.at[child, q], tf.at[child, r // 2], tf_send.at[child],
                    tf_recv.at[child], (q * 2 + co, c),
                ).start()

    def diagonal(child):
        wait_bytes(tf.at[child, pl.ds(0, 7)], tf_recv.at[child])
        total = tf[child, 0]
        for k in range(1, 8):
            total = total + tf[child, k]
        d_out[child] = binv[child] - total

    def a_sent():
        wait_bytes(a1.at[pl.ds(0, 30)], a1_send)

    def p_sent(child):
        wait_bytes(pg.at[c, child, pl.ds(0, 240), :], pa_send.at[child])
        wait_bytes(pg.at[pl.ds(0, 3), child], pz_send.at[child])
        wait_bytes(pg.at[pl.ds(0, 12), child], py_send.at[child])

    def r_sent(child):
        for item in (2 * child, 2 * child + 1):
            for layer in range(2):
                for j in range(4):
                    wait_bytes(sr.at[item, layer, j], sib_send.at[item, layer, j])
            if item in z_items:
                for j in range(4):
                    wait_bytes(zq.at[item, j], zq_send.at[item, j])
            else:
                wait_bytes(zs.at[item], z_send.at[item])
            for layer in (1,) if item in z_items else (0, 1):
                for side in range(2):
                    wait_bytes(x1.at[item, layer, side], x1_send.at[item, layer, side])
                    wait_bytes(x2.at[item, layer, side], x2_send.at[item, layer, side])

    def c_sent(child):
        c_wait(child, c1_send.at[child])

    def t_sent(child):
        for k in range(8):
            wait_bytes(tr.at[child, k], tr_send.at[child, k])
        wait_bytes(tf.at[child, pl.ds(0, 7)], tf_send.at[child])

    own()
    p_spread(0)
    p_spread(1)
    own_ready()
    p_gathered(0)
    p_z(0)
    p_y(0, 0)
    p_gathered(1)
    p_z(1)
    p_y_pass(0, 0)
    p_z_pass(0)
    a_spread()
    p_y(0, 1)
    p_y(0, 2)
    p_z_last(0)
    p_y(0, 3)
    p_y_pass(0, 1)
    p_y_pass(0, 2)
    p_y_pass(0, 3)
    p_y(1, 0)
    a_gathered()
    a_list(0)
    a_list(1)
    p_z_pass(1)
    p_y(1, 1)
    p_y(1, 2)
    p_ready(0)
    products(0, 0)
    x_first(0, 0)
    for j in (0, 1, 3, 2):
        z_send_on(1, j)
    products(0, 1)
    x_first(0, 1)
    x_first(1, 1)
    p_z_last(1)
    p_y(1, 3)
    p_y_pass(1, 0)
    x_second(0, 0)
    p_y_pass(1, 1)
    p_y_pass(1, 2)
    x_second(0, 1)
    x_second(1, 1)
    x_last(0, 0)
    p_y_pass(1, 3)
    x_last(0, 1)
    c_spread(0)
    x_last(1, 1)
    c_spread(1)
    p_ready(1)
    products_first(1)
    products(1, 1)
    x_first(2, 1)
    x_first(3, 1)
    x_second(2, 0)
    x_second(2, 1)
    x_second(3, 1)
    x_last(2, 0)
    x_last(2, 1)
    c_spread(2)
    x_last(3, 1)
    c_spread(3)
    c_ready(0)
    terms(0)
    terms_spread(0)
    diagonal(0)
    c_ready(1)
    terms(1)
    terms_spread(1)
    diagonal(1)

    a_sent()
    for child in range(2):
        p_sent(child)
        r_sent(child)
        c_sent(child)
        t_sent(child)


def body(root_inverse, panels, child_rows, block_inverse):
    vmem = pl.BlockSpec(memory_space=pltpu.VMEM)
    hbm = pl.BlockSpec(memory_space=pl.ANY)
    dma = pltpu.SemaphoreType.DMA
    coupling, diagonal = pl.pallas_call(
        kernel,
        out_shape=(
            jax.ShapeDtypeStruct((2, 2, BLOCK, 128), F32),
            jax.ShapeDtypeStruct((2, 128, 128), F32),
        ),
        in_specs=[pl.BlockSpec(memory_space=pltpu.SMEM), hbm, hbm, hbm],
        out_specs=(vmem, vmem),
        scratch_shapes=[
            pltpu.VMEM((2, 128, 128), F32),
            pltpu.VMEM((32, 16, 512), F32),
            pltpu.VMEM((2, 256, 512), F32),
            pltpu.VMEM((2, 512, 768), BF16),
            pltpu.VMEM((16, 2, 256, 128), F32),
            pltpu.VMEM((2, 8, 768, 256), BF16),
            pltpu.VMEM((4, 2, 4, 2, 256, 128), F32),
            pltpu.VMEM((4, 2, 4, 256, 128), F32),
            pltpu.VMEM((4, 2, 2, 128, 128), F32),
            pltpu.VMEM((4, 2, 2, 256, 128), F32),
            pltpu.VMEM((4, 256, 128), F32),
            pltpu.VMEM((4, 256, 128), F32),
            pltpu.VMEM((4, 4, 256, 128), F32),
            pltpu.VMEM((32, 16, 128), F32),
            pltpu.VMEM((32, 16, 128), F32),
            pltpu.VMEM((2, 256, 128), F32),
            pltpu.VMEM((2, 128, 768), BF16),
            pltpu.VMEM((2, 8, 2, 128, 128), F32),
            pltpu.VMEM((2, 8, 128, 128), F32),
            pltpu.VMEM((2, 8, 128, 128), F32),
            pltpu.VMEM((2, 8, 128, 128), F32),
            dma((4,)),
            dma, dma,
            dma((2,)), dma((2,)),
            dma((2,)), dma((2, 2)), dma((2, 2)),
            dma((2,)), dma((2, 4, 2)), dma((2, 4, 2)),
            dma((4, 2, 4)), dma((4, 2, 4)),
            dma((4, 2, 2)), dma((4, 2, 2)),
            dma((4, 2, 2)), dma((4, 2, 2)),
            dma((4,)), dma((4,)),
            dma((4, 4)), dma((4, 4)),
            dma((2,)), dma((2,)),
            dma((2, 8)), dma((2, 8)),
            dma((2,)), dma((2,)),
        ],
        compiler_params=pltpu.CompilerParams(
            collective_id=0, has_side_effects=True, vmem_limit_bytes=63 * 1024 * 1024
        ),
        cost_estimate=pl.CostEstimate(
            flops=3 * 2 * 2 * 256 * 2048 * (512 + 128), bytes_accessed=4 << 20, transcendentals=0
        ),
    )(child_rows, root_inverse.reshape(2, BLOCK, 512), panels, block_inverse)
    return coupling.reshape(2, 2 * BLOCK, 128), diagonal


def solution(mesh):
    in_specs = (P("pr", "pc"), P(None, "pr", "pc"), P(), P(None, "pc", "pr"))
    out_specs = (P(None, "pc", "pr"), P(None, "pc", "pr"))
    return jax.shard_map(body, mesh=mesh, in_specs=in_specs, out_specs=out_specs, check_vma=False)
```

```python
import jax
import jax.numpy as jnp
from jax import lax
from jax.experimental import pallas as pl
from jax.experimental.pallas import tpu as pltpu
from jax.sharding import PartitionSpec as P

BLOCK = 256
MESH = pl.DeviceIdType.MESH
F32 = jnp.float32
BF16 = jnp.bfloat16


def split(value):
    high = value.astype(BF16)
    low = (value - high.astype(F32)).astype(BF16)
    return high, low


def kernel(
    rows_ref, a_ref, p_ref, b_ref, c_out, d_out, binv,
    a1, a2, acat, pg, pcat, w, sr, x1, x2, zs, zr, zq,
    c1a, c1b, c2, ccat, tw, tr, ts, tf,
    own_sem, a1_send, a1_recv, pa_send, pa_recv, pz_send, pz_recv, pzh_recv,
    py_send, py_recv, pyh_recv,
    sib_send, sib_recv, x1_send, x1_recv, x2_send, x2_recv, z_send, z_recv, zq_send, zq_recv,
    c1_send, c1_recv, tr_send, tr_recv, tf_send, tf_recv,
):
    r = lax.axis_index("pr")
    c = lax.axis_index("pc")
    x, zl, co = r // 4, (r // 2) % 2, r % 2
    y, zh = c // 4, c % 4

    def chip(xx, zz, cc):
        return (xx * 4 + zz * 2 + cc, c)

    c1 = (c1a, c1b)
    zup, zdown = y * 4 + (zh + 1) % 4, y * 4 + (zh + 3) % 4
    yup, ydown = ((y + 1) % 4) * 4 + zh, ((y + 3) % 4) * 4 + zh
    places = (zh, (zh + 3) % 4, (zh + 1) % 4, (zh + 2) % 4)
    low_half, high_half = pl.ds(0, 128), pl.ds(128, 128)
    sibling = chip(x, zl, 1 - co)
    zpartner = chip(x, 1 - zl, co)
    xright = chip((x + 1) % 4, zl, co)
    xleft = chip((x + 3) % 4, zl, co)

    def remote(src, dst, send, recv, device):
        return pltpu.make_async_remote_copy(
            src_ref=src, dst_ref=dst, send_sem=send, recv_sem=recv,
            device_id=device, device_id_type=MESH,
        )

    def wait_bytes(ref, sem):
        pltpu.make_async_copy(ref, ref, sem).wait()

    barrier = pltpu.get_barrier_semaphore()

    def greet(k, carry):
        pl.semaphore_signal(barrier, inc=1, device_id=((r + k) % 16, c), device_id_type=MESH)
        return carry

    lax.fori_loop(1, 16, greet, 0)
    for plane in (zup, zdown, yup, ydown):
        pl.semaphore_signal(barrier, inc=1, device_id=(r, plane), device_id_type=MESH)

    pl.semaphore_wait(barrier, 19)

    def a_spread():
        lax.fori_loop(1, 16, a_spread_one, 0)

    def a_spread_one(k, carry):
        to = (r + k) % 16
        remote(
            a_ref.at[:, pl.ds(to * 16, 16), :], a1.at[pl.ds(r * 2, 2)],
            a1_send, a1_recv, (to, c),
        ).start()
        return carry


    def p_spread(child):
        def one(k, carry):
            to = (r + k) % 16
            remote(
                p_ref.at[child, pl.ds(to * 16, 16), :], pg.at[c, child, pl.ds(r * 16, 16), :],
                pa_send.at[child], pa_recv.at[child], (to, c),
            ).start()
            return carry

        lax.fori_loop(1, 16, one, 0)

    def p_gathered(child):
        wait_bytes(pg.at[c, child, pl.ds(0, 240), :], pa_recv.at[child])

    def send_piece(piece, child, to, send, recv):
        remote(pg.at[piece, child], pg.at[piece, child], send, recv, (r, to)).start()

    def send_half(piece, child, half, to, send, recv):
        ref = pg.at[piece, child, half, :]
        remote(ref, ref, send, recv, (r, to)).start()

    def p_z(child):
        send_piece(c, child, zup, pz_send.at[child], pz_recv.at[child, 0])
        send_piece(c, child, zdown, pz_send.at[child], pz_recv.at[child, 1])

    def p_y(child, k):
        piece = y * 4 + places[k]
        send_piece(piece, child, yup, py_send.at[child], py_recv.at[child, k, 0])
        send_piece(piece, child, ydown, py_send.at[child], py_recv.at[child, k, 1])

    def p_z_pass(child):
        wait_bytes(pg.at[zdown, child], pz_recv.at[child, 0])
        send_half(zdown, child, low_half, zup, pz_send.at[child], pzh_recv.at[child, 0])
        wait_bytes(pg.at[zup, child], pz_recv.at[child, 1])
        send_half(zup, child, high_half, zdown, pz_send.at[child], pzh_recv.at[child, 1])

    def p_z_last(child):
        piece = y * 4 + places[3]
        wait_bytes(pg.at[piece, child, low_half, :], pzh_recv.at[child, 0])
        wait_bytes(pg.at[piece, child, high_half, :], pzh_recv.at[child, 1])

    def p_y_pass(child, k):
        below, above = ((y + 3) % 4) * 4 + places[k], ((y + 1) % 4) * 4 + places[k]
        wait_bytes(pg.at[below, child], py_recv.at[child, k, 0])
        send_half(below, child, low_half, yup, py_send.at[child], pyh_recv.at[child, k, 0])
        wait_bytes(pg.at[above, child], py_recv.at[child, k, 1])
        send_half(above, child, high_half, ydown, py_send.at[child], pyh_recv.at[child, k, 1])

    def p_y_last(child, k):
        piece = ((y + 2) % 4) * 4 + places[k]
        wait_bytes(pg.at[piece, child, low_half, :], pyh_recv.at[child, k, 0])
        wait_bytes(pg.at[piece, child, high_half, :], pyh_recv.at[child, k, 1])

    a_own = pltpu.make_async_copy(
        a_ref.at[:, pl.ds(r * 16, 16), :], a1.at[pl.ds(r * 2, 2)], own_sem.at[0]
    )
    p_mine = [
        pltpu.make_async_copy(
            p_ref.at[child, pl.ds(r * 16, 16), :], pg.at[c, child, pl.ds(r * 16, 16), :],
            own_sem.at[1 + child],
        )
        for child in range(2)
    ]

    b_own = pltpu.make_async_copy(b_ref, binv, own_sem.at[3])

    def own():
        for copy in (p_mine[0], p_mine[1], a_own, b_own):
            copy.start()

    def own_ready():
        for copy in (p_mine[0], p_mine[1], a_own, b_own):
            copy.wait()

    def a_gathered():
        wait_bytes(a1.at[pl.ds(0, 30)], a1_recv)

    def a_list(child):
        for t in range(16):
            a2[child, t * 16:(t + 1) * 16, :] = -a1[rows_ref[child, t]]
        high, low = split(a2[child].T)
        acat[child, :, 0:256] = high
        acat[child, :, 256:512] = high
        acat[child, :, 512:768] = low

    def p_ready(child):
        for k in range(4):
            p_y_last(child, k)

        def pair(q, carry):
            for half in range(2):
                lanes = pl.ds(half * 128, 128)
                high, low = split(pg[q * 2 + half, child])
                pcat[child, q, 0:256, lanes] = high
                pcat[child, q, 256:512, lanes] = low
                pcat[child, q, 512:768, lanes] = high
            return carry

        lax.fori_loop(0, 8, pair, 0)

    z_items = (1, 3)

    def products(child, layer):
        def one(j, carry):
            product(child, layer, j)
            return carry

        lax.fori_loop(0, 4, one, 0)

    def product(child, layer, j):
        q = ((x + 6 - j) % 4) * 2 + (zl + 1 + layer) % 2
        result = jnp.dot(acat[child], pcat[child, q], preferred_element_type=F32)
        for block in range(2):
            item = 2 * child + block
            rows = slice(block * 256, block * 256 + 256)
            w[item, layer, j, 0] = result[rows, 0:128]
            w[item, layer, j, 1] = result[rows, 128:256]
            remote(
                w.at[item, layer, j, 1 - co], sr.at[item, layer, j], sib_send.at[item, layer, j],
                sib_recv.at[item, layer, j], sibling,
            ).start()

    def products_first(child):
        block_x, block_z = 2 * child, 2 * child + 1
        last = None
        for j in (0, 1, 3, 2):
            product(child, 0, j)
            if last is not None:
                z_send_on(block_z, last)
            if j == 3:
                x_first(block_x, 0)
            last = j
        z_send_on(block_z, last)

    def chip_sum(item, layer, j):
        wait_bytes(sr.at[item, layer, j], sib_recv.at[item, layer, j])
        total = sr[item, layer, j] + w[item, layer, j, co]
        if item in z_items and layer == 1:
            wait_bytes(zq.at[item, j], zq_recv.at[item, j])
            total = total + zq[item, j]
        sr[item, layer, j] = total

    def z_send_on(item, j):
        chip_sum(item, 0, j)
        remote(
            sr.at[item, 0, j], zq.at[item, j], zq_send.at[item, j], zq_recv.at[item, j], zpartner
        ).start()

    def x_first(item, layer):
        chip_sum(item, layer, 0)
        for side, rows, to in ((0, pl.ds(0, 128), xright), (1, pl.ds(128, 128), xleft)):
            remote(
                sr.at[item, layer, 0, rows, :], x1.at[item, layer, side],
                x1_send.at[item, layer, side], x1_recv.at[item, layer, side], to,
            ).start()

    def x_second(item, layer):
        for side, j, to in ((0, 1, xright), (1, 3, xleft)):
            chip_sum(item, layer, j)
            rows = slice(side * 128, side * 128 + 128)
            wait_bytes(x1.at[item, layer, side], x1_recv.at[item, layer, side])
            sr[item, layer, j, rows, :] = sr[item, layer, j, rows, :] + x1[item, layer, side]
            remote(
                sr.at[item, layer, j], x2.at[item, layer, side],
                x2_send.at[item, layer, side], x2_recv.at[item, layer, side], to,
            ).start()

    def x_last(item, layer):
        chip_sum(item, layer, 2)
        for side in range(2):
            wait_bytes(x2.at[item, layer, side], x2_recv.at[item, layer, side])
        total = sr[item, layer, 2] + x2[item, layer, 0] + x2[item, layer, 1]
        if layer == 0:
            zs[item] = total
            remote(zs.at[item], zr.at[item], z_send.at[item], z_recv.at[item], zpartner).start()
        else:
            if item not in z_items:
                wait_bytes(zr.at[item], z_recv.at[item])
                total = total + zr[item]
            c_out[item // 2, item % 2] = total

    def c_spread(item):
        child, block = item // 2, item % 2

        def one(k, carry):
            u = (c + k) % 16
            source = c_out.at[child, block, pl.ds(u * 16, 16), :]
            target = c1[child].at[c * 2 + block]

            @pl.when((r != c) | (u != r))
            def _():
                remote(source, target, c1_send.at[child], c1_recv.at[child], (u, r)).start()

            return carry

        lax.fori_loop(0, 16, one, 0)

        @pl.when(r == c)
        def _():
            c1[child][c * 2 + block] = c_out[child, block, pl.ds(r * 16, 16), :]

    def c_wait(child, sem):
        @pl.when(r == c)
        def _():
            wait_bytes(c1[child].at[pl.ds(0, 30)], sem)

        @pl.when(r != c)
        def _():
            wait_bytes(c1[child], sem)

    def c_ready(child):
        c_wait(child, c1_recv.at[child])
        for t in range(16):
            c2[child, t * 16:(t + 1) * 16, :] = c1[child][rows_ref[child, t]]

    def terms(child):
        high, low = split(c2[child].T)
        ccat[child, :, 0:256] = high
        ccat[child, :, 256:512] = high
        ccat[child, :, 512:768] = low

        def one(k, carry):
            q = term_place(k)
            result = jnp.dot(ccat[child], pcat[child, q], preferred_element_type=F32)
            tw[child, q, 0] = result[:, 0:128]
            tw[child, q, 1] = result[:, 128:256]
            remote(
                tw.at[child, q, 1 - co], tr.at[child, q], tr_send.at[child, k],
                tr_recv.at[child, k], sibling,
            ).start()
            return carry

        lax.fori_loop(0, 8, one, 0)

    def term_place(k):
        return ((x + 2 + k) % 4) * 2 + (zl + 1 + k // 4) % 2

    def terms_spread(child):
        for k in (0, 1, 3, 2, 4, 5, 7, 6):
            q = term_place(k)
            wait_bytes(tr.at[child, q], tr_recv.at[child, k])
            total = tw[child, q, co] + tr[child, q]
            if k == 6:
                tf[child, r // 2] = total
            else:
                ts[child, q] = total
                remote(
                    ts.at[child, q], tf.at[child, r // 2], tf_send.at[child],
                    tf_recv.at[child], (q * 2 + co, c),
                ).start()

    def diagonal(child):
        wait_bytes(tf.at[child, pl.ds(0, 7)], tf_recv.at[child])
        total = tf[child, 0]
        for k in range(1, 8):
            total = total + tf[child, k]
        d_out[child] = binv[child] - total

    def a_sent():
        wait_bytes(a1.at[pl.ds(0, 30)], a1_send)

    def p_sent(child):
        wait_bytes(pg.at[c, child, pl.ds(0, 240), :], pa_send.at[child])
        wait_bytes(pg.at[pl.ds(0, 3), child], pz_send.at[child])
        wait_bytes(pg.at[pl.ds(0, 12), child], py_send.at[child])

    def r_sent(child):
        for item in (2 * child, 2 * child + 1):
            for layer in range(2):
                for j in range(4):
                    wait_bytes(sr.at[item, layer, j], sib_send.at[item, layer, j])
            if item in z_items:
                for j in range(4):
                    wait_bytes(zq.at[item, j], zq_send.at[item, j])
            else:
                wait_bytes(zs.at[item], z_send.at[item])
            for layer in (1,) if item in z_items else (0, 1):
                for side in range(2):
                    wait_bytes(x1.at[item, layer, side], x1_send.at[item, layer, side])
                    wait_bytes(x2.at[item, layer, side], x2_send.at[item, layer, side])

    def c_sent(child):
        c_wait(child, c1_send.at[child])

    def t_sent(child):
        for k in range(8):
            wait_bytes(tr.at[child, k], tr_send.at[child, k])
        wait_bytes(tf.at[child, pl.ds(0, 7)], tf_send.at[child])

    own()
    p_spread(0)
    p_spread(1)
    own_ready()
    p_gathered(0)
    p_z(0)
    p_y(0, 0)
    p_gathered(1)
    p_z(1)
    p_y_pass(0, 0)
    p_z_pass(0)
    a_spread()
    p_y(0, 1)
    p_y(0, 2)
    p_z_last(0)
    p_y(0, 3)
    p_y_pass(0, 1)
    p_y_pass(0, 2)
    p_y_pass(0, 3)
    p_y(1, 0)
    a_gathered()
    a_list(0)
    a_list(1)
    p_z_pass(1)
    p_y(1, 1)
    p_y(1, 2)
    p_ready(0)
    products(0, 0)
    x_first(0, 0)
    for j in (0, 1, 3, 2):
        z_send_on(1, j)
    products(0, 1)
    x_first(0, 1)
    x_first(1, 1)
    p_z_last(1)
    p_y(1, 3)
    p_y_pass(1, 0)
    x_second(0, 0)
    p_y_pass(1, 1)
    p_y_pass(1, 2)
    x_second(0, 1)
    x_second(1, 1)
    p_y_pass(1, 3)
    x_last(0, 0)
    x_last(0, 1)
    c_spread(0)
    x_last(1, 1)
    c_spread(1)
    p_ready(1)
    products_first(1)
    products(1, 1)
    x_first(2, 1)
    x_first(3, 1)
    x_second(2, 0)
    x_second(2, 1)
    x_second(3, 1)
    x_last(2, 0)
    x_last(2, 1)
    c_spread(2)
    x_last(3, 1)
    c_spread(3)
    c_ready(0)
    terms(0)
    terms_spread(0)
    diagonal(0)
    c_ready(1)
    terms(1)
    terms_spread(1)
    diagonal(1)

    a_sent()
    for child in range(2):
        p_sent(child)
        r_sent(child)
        c_sent(child)
        t_sent(child)


def body(root_inverse, panels, child_rows, block_inverse):
    vmem = pl.BlockSpec(memory_space=pltpu.VMEM)
    hbm = pl.BlockSpec(memory_space=pl.ANY)
    dma = pltpu.SemaphoreType.DMA
    coupling, diagonal = pl.pallas_call(
        kernel,
        out_shape=(
            jax.ShapeDtypeStruct((2, 2, BLOCK, 128), F32),
            jax.ShapeDtypeStruct((2, 128, 128), F32),
        ),
        in_specs=[pl.BlockSpec(memory_space=pltpu.SMEM), hbm, hbm, hbm],
        out_specs=(vmem, vmem),
        scratch_shapes=[
            pltpu.VMEM((2, 128, 128), F32),
            pltpu.VMEM((32, 16, 512), F32),
            pltpu.VMEM((2, 256, 512), F32),
            pltpu.VMEM((2, 512, 768), BF16),
            pltpu.VMEM((16, 2, 256, 128), F32),
            pltpu.VMEM((2, 8, 768, 256), BF16),
            pltpu.VMEM((4, 2, 4, 2, 256, 128), F32),
            pltpu.VMEM((4, 2, 4, 256, 128), F32),
            pltpu.VMEM((4, 2, 2, 128, 128), F32),
            pltpu.VMEM((4, 2, 2, 256, 128), F32),
            pltpu.VMEM((4, 256, 128), F32),
            pltpu.VMEM((4, 256, 128), F32),
            pltpu.VMEM((4, 4, 256, 128), F32),
            pltpu.VMEM((32, 16, 128), F32),
            pltpu.VMEM((32, 16, 128), F32),
            pltpu.VMEM((2, 256, 128), F32),
            pltpu.VMEM((2, 128, 768), BF16),
            pltpu.VMEM((2, 8, 2, 128, 128), F32),
            pltpu.VMEM((2, 8, 128, 128), F32),
            pltpu.VMEM((2, 8, 128, 128), F32),
            pltpu.VMEM((2, 8, 128, 128), F32),
            dma((4,)),
            dma, dma,
            dma((2,)), dma((2,)),
            dma((2,)), dma((2, 2)), dma((2, 2)),
            dma((2,)), dma((2, 4, 2)), dma((2, 4, 2)),
            dma((4, 2, 4)), dma((4, 2, 4)),
            dma((4, 2, 2)), dma((4, 2, 2)),
            dma((4, 2, 2)), dma((4, 2, 2)),
            dma((4,)), dma((4,)),
            dma((4, 4)), dma((4, 4)),
            dma((2,)), dma((2,)),
            dma((2, 8)), dma((2, 8)),
            dma((2,)), dma((2,)),
        ],
        compiler_params=pltpu.CompilerParams(
            collective_id=0, has_side_effects=True, vmem_limit_bytes=63 * 1024 * 1024
        ),
        cost_estimate=pl.CostEstimate(
            flops=3 * 2 * 2 * 256 * 2048 * (512 + 128), bytes_accessed=4 << 20, transcendentals=0
        ),
    )(child_rows, root_inverse.reshape(2, BLOCK, 512), panels, block_inverse)
    return coupling.reshape(2, 2 * BLOCK, 128), diagonal


def solution(mesh):
    in_specs = (P("pr", "pc"), P(None, "pr", "pc"), P(), P(None, "pc", "pr"))
    out_specs = (P(None, "pc", "pr"), P(None, "pc", "pr"))
    return jax.shard_map(body, mesh=mesh, in_specs=in_specs, out_specs=out_specs, check_vma=False)
```
